512 devices in a mesh: ctx: 8 (over z_lo, core), ch: 64 (over z_hi, x, y).
Axes of the slice: x: 4, y: 8, z: 8 (z_hi: 2, z_lo: 4; z = z_hi * 4 + z_lo), core: 2. Of those that a mesh axis runs over, the one named last changes fastest.
Arguments:
- mamba_in: bfloat16 [4096, 16384], P('ctx', 'ch'), may hold values from -6 to 6
- mamba_gate: bfloat16 [4096, 16384], P('ctx', 'ch'), may hold values from -6 to 6
- conv_weight: float32 [4, 16384], P(None, 'ch'), may hold values from -3 to 3
- conv_bias: float32 [16384], P('ch'), may hold values from -0.5 to 0.5
- proj_delta: bfloat16 [16384, 512], P('ch'), may hold values from -0.046875 to 0.046875
- proj_select: bfloat16 [16384, 32], P('ch'), may hold values from -0.046875 to 0.046875
- delta_weight: bfloat16 [512, 16384], P(None, 'ch'), may hold values from -0.25 to 0.25
- delta_bias: float32 [16384], P('ch'), may hold values from -4.6 to -2.3
- decay_log: float32 [16, 16384], P(None, 'ch'), may hold values from -9 to 0
- skip_gain: float32 [16384], P('ch'), may hold values from 0.5 to 1.5
Outputs:
- mamba_out: bfloat16 [4096, 16384], P('ctx', 'ch')
The draws below stay inside these ranges and needn't reach their ends.
All inputs are finite; a program needn't handle non-finite values.
Results may differ from the reference program's by a relative error of at most 0.0051.
Values may be sent and summed in bfloat16 or wider, within the bound.
No kernel may reach another device: no remote copies, remote signals or barrier semaphores. Data moves between devices by JAX's collectives and lax.ppermute only.
A program may use at most 64 MiB of HBM per device.

```python
import jax
import jax.numpy as jnp
from jax import lax

INNER = 16384
RANK = 512
STATE = 16
KWIDTH = 4
SEQ = 4096


def shard_levels(stream_key, shape, pieces, least, high):
    def one(position, shards_of):
        heights = jax.random.uniform(jax.random.fold_in(jax.random.fold_in(stream_key, 6), position), (shards_of,), jnp.float32, least / len(pieces), high / len(pieces))
        return jnp.repeat(jnp.exp(heights), shape[position] // shards_of).reshape((-1,) + (1,) * (len(shape) - position - 1))

    level = one(*pieces[0])
    for cut in pieces[1:]:
        level = level * one(*cut)
    return level


def noise(key, shape, deviation, reach, split=(), kind=jnp.bfloat16):
    factor_of = shard_levels(key, shape, split, -0.22, 0.18) if split else 1.0
    drawn = jax.random.normal(key, shape, jnp.float32) * deviation * factor_of
    return jnp.minimum(jnp.maximum(drawn, -reach), reach).astype(kind)


def setup_inputs(seed: int = 0) -> dict:
    keys = jax.random.split(jax.random.key(seed), 11)
    mamba_in = noise(keys[0], (SEQ, INNER), 1.0, 6.0, ((0, 8), (1, 64)))
    mamba_gate = noise(keys[1], (SEQ, INNER), 1.0, 6.0, ((0, 8), (1, 64)))
    conv_weight = noise(keys[2], (KWIDTH, INNER), KWIDTH ** -0.5, 3.0, ((1, 64),), jnp.float32)
    conv_bias = jnp.clip(jax.random.uniform(keys[3], (INNER,), jnp.float32, -0.5, 0.5) * shard_levels(keys[3], (INNER,), ((0, 64),), -0.4, 0.0), -0.5, 0.5)
    proj_delta = noise(keys[4], (INNER, RANK), INNER ** -0.5, 0.046875, ((0, 64),))
    proj_select = noise(keys[5], (INNER, 2 * STATE), INNER ** -0.5, 0.046875, ((0, 64),))
    delta_weight = noise(keys[6], (RANK, INNER), RANK ** -0.5, 0.25, ((1, 64),))
    delta_bias = jnp.clip(-4.6 + 2.3 * jax.random.uniform(keys[7], (INNER,), jnp.float32) ** shard_levels(keys[7], (INNER,), ((0, 64),), -0.2, 0.2), -4.6, -2.3)
    decay_log = jnp.clip(-9.0 + 9.0 * jax.random.uniform(keys[8], (STATE, INNER), jnp.float32) ** shard_levels(keys[8], (STATE, INNER), ((1, 64),), -0.2, 0.2), -9.0, 0.0)
    skip_gain = jnp.clip(0.5 + 1.0 * jax.random.uniform(keys[9], (INNER,), jnp.float32) ** shard_levels(keys[9], (INNER,), ((0, 64),), -0.2, 0.2), 0.5, 1.5)
    return dict(mamba_in=mamba_in, mamba_gate=mamba_gate, conv_weight=conv_weight, conv_bias=conv_bias, proj_delta=proj_delta, proj_select=proj_select, delta_weight=delta_weight, delta_bias=delta_bias, decay_log=decay_log, skip_gain=skip_gain)


def reference(mamba_in, mamba_gate, conv_weight, conv_bias, proj_delta, proj_select, delta_weight, delta_bias, decay_log, skip_gain):
    padded = jnp.concatenate([jnp.zeros((KWIDTH - 1, INNER), mamba_in.dtype), mamba_in], axis=0)
    conv_sum = conv_bias[None, :]
    for offset in range(KWIDTH):
        conv_sum = conv_sum + conv_weight[offset][None, :] * padded[offset:offset + SEQ].astype(jnp.float32)
    inner_act = jax.nn.silu(conv_sum)
    inner_low = inner_act.astype(jnp.bfloat16)
    delta_low = jnp.dot(inner_low, proj_delta, preferred_element_type=jnp.float32)
    selected = jnp.dot(inner_low, proj_select, preferred_element_type=jnp.float32)
    delta_rate = jax.nn.softplus(jnp.dot(delta_low.astype(jnp.bfloat16), delta_weight, preferred_element_type=jnp.float32) + delta_bias[None, :])
    decay_rate = -jnp.exp(decay_log)

    def advance(state_now, row_inputs):
        delta_row, inner_row, b_row, c_row = row_inputs
        state_now = jnp.exp(delta_row[None, :] * decay_rate) * state_now + (delta_row * inner_row)[None, :] * b_row[:, None]
        return state_now, jnp.sum(c_row[:, None] * state_now, axis=0)

    ignored, scanned = lax.scan(advance, jnp.zeros((STATE, INNER), jnp.float32), (delta_rate, inner_act, selected[:, :STATE], selected[:, STATE:]))
    scan_out = scanned + skip_gain[None, :] * inner_act
    return (scan_out * jax.nn.silu(mamba_gate.astype(jnp.float32))).astype(jnp.bfloat16)
```

```python
import functools
import math

import jax
import jax.numpy as jnp
from jax import lax
from jax.experimental import pallas as pl
from jax.experimental.pallas import tpu as pltpu
from jax.sharding import PartitionSpec as P

STATE = 16
KWIDTH = 4
LANES = 128
CHUNKS = 8
LOG2E = 1.0 / math.log(2.0)
MIB = 1 << 20
F32 = jnp.float32
BF16 = jnp.bfloat16


def vmem(count):
    return [pl.BlockSpec(memory_space=pltpu.VMEM)] * count


def project_kernel(x_ref, halo_ref, weight_ref, bias_ref, pd_ref, ps_ref, act_ref, part_ref, xs, xp, low, sel):
    rows, width = x_ref.shape
    steps = rows // CHUNKS
    rank = pd_ref.shape[1]
    halves = width // LANES
    for half in range(halves):
        cols = slice(half * LANES, (half + 1) * LANES)
        xs[half, 0:8, :] = halo_ref[...].astype(F32)[-8:, cols]
        xs[half, 8 : 8 + rows, :] = x_ref[:, cols].astype(F32)
        for step in range(-(KWIDTH - 1), steps):
            to = (step + KWIDTH - 1) * CHUNKS
            xp[half, to : to + CHUNKS, :] = xs[half, pl.ds(8 + step, CHUNKS, stride=steps), :]
    block = min(rows, 64)
    for half in range(halves):
        cols = slice(half * LANES, (half + 1) * LANES)
        for start in range(0, rows, block):
            value = bias_ref[:, cols]
            for tap in range(KWIDTH):
                at = start + tap * CHUNKS
                value = value + weight_ref[tap : tap + 1, cols] * xp[half, at : at + block, :]
            value = value / (1.0 + jnp.exp(-value))
            act_ref[start : start + block, cols] = value
            low[start : start + block, cols] = value.astype(BF16)
    maps = ps_ref.shape[1]
    sel[...] = jnp.zeros_like(sel)
    sel[:, 0:maps] = ps_ref[...]
    sel[:, maps : 2 * maps] = ps_ref[...]
    part_ref[:, 0:rank] = jnp.dot(low[...], pd_ref[...], preferred_element_type=F32).astype(BF16)
    both = jnp.dot(low[...], sel[...], preferred_element_type=F32)
    high = both.astype(BF16)
    rest = (both - high.astype(F32)).astype(BF16)
    lane = lax.broadcasted_iota(jnp.int32, both.shape, 1)
    part_ref[:, rank : rank + LANES] = jnp.where(lane < maps, high.astype(F32), rest.astype(F32)).astype(BF16)


def total_kernel(rank, maps, parts_ref, out_ref):
    devices, rows, width = parts_ref.shape
    total = parts_ref[0].astype(F32)
    for source in range(1, devices):
        total = total + parts_ref[source].astype(F32)
    chosen = total[:, rank:]
    lane = lax.broadcasted_iota(jnp.int32, chosen.shape, 1)
    summed = chosen + pltpu.roll(chosen, LANES - maps, 1)
    twice = jnp.where(lane < maps, summed, pltpu.roll(summed, maps, 1))
    high = twice.astype(BF16).astype(F32)
    rest = jnp.where(lane < 2 * maps, twice - high, 0.0)
    mixed = jnp.where(lane < maps, high, rest)
    row = jnp.concatenate([total[:, :rank], mixed], axis=1).astype(BF16)
    for target in range(devices):
        out_ref[target] = row


def spread(first, maps):
    shape = (LANES, STATE * LANES)
    source = lax.broadcasted_iota(jnp.int32, shape, 0)
    group = lax.broadcasted_iota(jnp.int32, shape, 1) >> 7
    hit = (source == group + first) | (source == group + (first + maps))
    return jnp.where(hit, 1.0, 0.0).astype(BF16)


def scan_kernel(
    rank, me_ref, g_ref, act_ref, dw_ref, bias_ref, log_ref,
    y_ref, cum_ref, inside_ref, before_ref, pay_ref,
    delta, drive, b_all, c_all, rate, ends,
):
    rows, width = act_ref.shape
    steps = rows // CHUNKS
    halves = width // LANES
    maps = 2 * STATE
    z = jnp.dot(g_ref[:, :rank], dw_ref[...], preferred_element_type=F32) + bias_ref[...]
    step_size = jnp.maximum(z, 0.0) + jnp.log1p(jnp.exp(-jnp.abs(z)))
    delta[...] = step_size
    drive[...] = step_size * act_ref[...]
    b_all[...] = jnp.dot(g_ref[:, rank:], spread(0, maps), preferred_element_type=F32)
    c_all[...] = jnp.dot(g_ref[:, rank:], spread(STATE, maps), preferred_element_type=F32)
    rate[...] = -jnp.exp(log_ref[...]) * LOG2E
    chunk = lax.broadcasted_iota(jnp.int32, (CHUNKS, LANES), 0)

    for half in range(halves):
        cols = slice(half * LANES, (half + 1) * LANES)
        rates = [jnp.broadcast_to(rate[n : n + 1, cols], (CHUNKS, LANES)) for n in range(STATE)]

        def advance(step, carried, cols=cols, rates=rates):
            states, total = carried
            at = pl.ds(pl.multiple_of(step * CHUNKS, CHUNKS), CHUNKS)
            size = delta[at, cols]
            push = drive[at, cols]
            total = total + size
            out = jnp.zeros((CHUNKS, LANES), F32)
            later = []
            for n in range(STATE):
                group = slice(n * LANES, (n + 1) * LANES)
                now = jnp.exp2(size * rates[n]) * states[n] + push * b_all[at, group]
                out = out + c_all[at, group] * now
                later.append(now)
            y_ref[at, cols] = out
            cum_ref[at, cols] = total
            return later, total

        zero = jnp.zeros((CHUNKS, LANES), F32)
        states, total = lax.fori_loop(0, steps, advance, ([zero] * STATE, zero))
        sums = [total]
        shift = 1
        while shift < CHUNKS:
            sums.append(sums[-1] + jnp.where(chunk >= shift, pltpu.roll(sums[-1], shift, 0), 0.0))
            shift *= 2
        for n in range(STATE):
            end = states[n]
            shift = 1
            for level in range(len(sums) - 1):
                end = end + jnp.exp2(rates[n] * sums[level]) * jnp.where(
                    chunk >= shift, pltpu.roll(end, shift, 0), 0.0
                )
                shift *= 2
            inside_ref[n, :, cols] = jnp.where(chunk >= 1, pltpu.roll(end, 1, 0), 0.0)
            ends[n : n + 1, cols] = end[CHUNKS - 1 :, :]
        before_ref[:, cols] = jnp.where(chunk >= 1, pltpu.roll(sums[-1], 1, 0), 0.0)
        ends[STATE : STATE + 1, cols] = sums[-1][CHUNKS - 1 :, :]

    me = me_ref[0]
    value = ends[0:STATE, :]
    high = value.astype(BF16).astype(F32)
    total = jnp.broadcast_to(ends[STATE : STATE + 1, :], value.shape)
    total_high = total.astype(BF16).astype(F32)
    first = lax.broadcasted_iota(jnp.int32, value.shape, 0) == 0
    tail = jnp.where(first, total_high, total - total_high)
    for target in range(pay_ref.shape[0]):
        use = target > me
        pay_ref[target, 0:16, :] = jnp.where(use, high, 0.0).astype(BF16)
        pay_ref[target, 16:32, :] = jnp.where(use, value - high, 0.0).astype(BF16)
        pay_ref[target, 32:48, :] = jnp.where(use, tail, 0.0).astype(BF16)


def finish_kernel(
    rank, got_ref, g_ref, act_ref, y_ref, cum_ref, inside_ref, before_ref, log_ref, gain_ref, gate_ref,
    out_ref, c_all, rate, carry, ys,
):
    rows, width = act_ref.shape
    steps = rows // CHUNKS
    halves = width // LANES
    c_all[...] = jnp.dot(g_ref[:, rank:], spread(STATE, 2 * STATE), preferred_element_type=F32)
    rate[...] = -jnp.exp(log_ref[...]) * LOG2E
    incoming = jnp.zeros((STATE, width), F32)
    for source in range(got_ref.shape[0] - 1):
        value = got_ref[source, 0:16, :].astype(F32) + got_ref[source, 16:32, :].astype(F32)
        tail = got_ref[source, 32:48, :].astype(F32)
        incoming = jnp.exp2(rate[...] * (tail[0:1, :] + tail[1:2, :])) * incoming + value
    carry[...] = incoming
    for half in range(halves):
        cols = slice(half * LANES, (half + 1) * LANES)
        rates = [jnp.broadcast_to(rate[n : n + 1, cols], (CHUNKS, LANES)) for n in range(STATE)]
        before = before_ref[:, cols]
        entering = [
            inside_ref[n, :, cols] + jnp.exp2(rates[n] * before) * carry[n : n + 1, cols] for n in range(STATE)
        ]
        gain = gain_ref[:, cols]

        def correct(step, _, half=half, cols=cols, rates=rates, entering=entering, gain=gain):
            at = pl.ds(pl.multiple_of(step * CHUNKS, CHUNKS), CHUNKS)
            total = cum_ref[at, cols]
            out = y_ref[at, cols] + gain * act_ref[at, cols]
            for n in range(STATE):
                group = slice(n * LANES, (n + 1) * LANES)
                out = out + (c_all[at, group] * entering[n]) * jnp.exp2(total * rates[n])
            ys[half, pl.ds(step, CHUNKS, stride=steps), :] = out
            return 0

        lax.fori_loop(0, steps, correct, 0)
        gate = gate_ref[:, cols].astype(F32)
        out_ref[:, cols] = (ys[half] * (gate / (1.0 + jnp.exp(-gate)))).astype(BF16)


def on_device(
    mamba_in, mamba_gate, conv_weight, conv_bias, proj_delta, proj_select, delta_weight, delta_bias, decay_log, skip_gain,
):
    rows, width = mamba_in.shape
    rank = proj_delta.shape[1]
    maps = proj_select.shape[1]
    halves = width // LANES
    steps = rows // CHUNKS
    n_ctx, n_ch = lax.axis_size("ctx"), lax.axis_size("ch")
    wide = rank + LANES
    me = lax.axis_index("ctx").astype(jnp.int32).reshape(1)

    halo = lax.ppermute(mamba_in[rows - 16 :], "ctx", [(i, i + 1) for i in range(n_ctx - 1)])
    act, part = pl.pallas_call(
        project_kernel,
        out_shape=(
            jax.ShapeDtypeStruct((rows, width), F32),
            jax.ShapeDtypeStruct((rows, wide), BF16),
        ),
        in_specs=vmem(6),
        out_specs=tuple(vmem(2)),
        scratch_shapes=[
            pltpu.VMEM((halves, rows + 8, LANES), F32),
            pltpu.VMEM((halves, (steps + KWIDTH - 1) * CHUNKS, LANES), F32),
            pltpu.VMEM((rows, width), BF16),
            pltpu.VMEM((width, LANES), BF16),
        ],
        compiler_params=pltpu.CompilerParams(vmem_limit_bytes=16 * MIB),
        name="project",
    )(mamba_in, halo, conv_weight, conv_bias[None, :], proj_delta, proj_select)

    parts = lax.all_to_all(part.reshape(n_ch, rows // n_ch, wide), "ch", 0, 0)
    totals = pl.pallas_call(
        functools.partial(total_kernel, rank, maps),
        out_shape=jax.ShapeDtypeStruct(parts.shape, BF16),
        in_specs=vmem(1),
        out_specs=vmem(1)[0],
        compiler_params=pltpu.CompilerParams(vmem_limit_bytes=16 * MIB),
        name="total",
    )(parts)
    gathered = lax.all_to_all(totals, "ch", 0, 0).reshape(rows, wide)

    y_local, cum, inside, before, pay = pl.pallas_call(
        functools.partial(scan_kernel, rank),
        out_shape=(
            jax.ShapeDtypeStruct((rows, width), F32),
            jax.ShapeDtypeStruct((rows, width), F32),
            jax.ShapeDtypeStruct((STATE, CHUNKS, width), F32),
            jax.ShapeDtypeStruct((CHUNKS, width), F32),
            jax.ShapeDtypeStruct((n_ctx, 3 * STATE, width), BF16),
        ),
        in_specs=[pl.BlockSpec(memory_space=pltpu.SMEM)] + vmem(5),
        out_specs=tuple(vmem(5)),
        scratch_shapes=[
            pltpu.VMEM((rows, width), F32),
            pltpu.VMEM((rows, width), F32),
            pltpu.VMEM((rows, STATE * LANES), F32),
            pltpu.VMEM((rows, STATE * LANES), F32),
            pltpu.VMEM((STATE, width), F32),
            pltpu.VMEM((STATE + 8, width), F32),
        ],
        compiler_params=pltpu.CompilerParams(vmem_limit_bytes=24 * MIB),
        name="local_scan",
    )(me, gathered, act, delta_weight, delta_bias[None, :], decay_log)

    got = lax.all_to_all(pay, "ctx", 0, 0)
    return pl.pallas_call(
        functools.partial(finish_kernel, rank),
        out_shape=jax.ShapeDtypeStruct((rows, width), BF16),
        in_specs=vmem(10),
        out_specs=vmem(1)[0],
        scratch_shapes=[
            pltpu.VMEM((rows, STATE * LANES), F32),
            pltpu.VMEM((STATE, width), F32),
            pltpu.VMEM((STATE, width), F32),
            pltpu.VMEM((halves, rows, LANES), F32),
        ],
        compiler_params=pltpu.CompilerParams(vmem_limit_bytes=24 * MIB),
        name="finish",
    )(got, gathered, act, y_local, cum, inside, before, decay_log, skip_gain[None, :], mamba_gate)


def solution(mesh):
    return jax.shard_map(
        on_device,
        mesh=mesh,
        in_specs=(
            P("ctx", "ch"),
            P("ctx", "ch"),
            P(None, "ch"),
            P("ch"),
            P("ch", None),
            P("ch", None),
            P(None, "ch"),
            P("ch"),
            P(None, "ch"),
            P("ch"),
        ),
        out_specs=P("ctx", "ch"),
        check_vma=False,
    )
```

```python
import functools
import math

import jax
import jax.numpy as jnp
from jax import lax
from jax.experimental import pallas as pl
from jax.experimental.pallas import tpu as pltpu
from jax.sharding import PartitionSpec as P

STATE = 16
KWIDTH = 4
LANES = 128
CHUNKS = 8
HEAD = 32
LOG2E = 1.0 / math.log(2.0)
MIB = 1 << 20
F32 = jnp.float32
BF16 = jnp.bfloat16


def vmem(count):
    return [pl.BlockSpec(memory_space=pltpu.VMEM)] * count


def hbm(count):
    return [pl.BlockSpec(memory_space=pltpu.HBM)] * count


def stay(*arrays):
    return [pltpu.with_memory_space_constraint(array, pltpu.HBM) for array in arrays]


def silu(value):
    return value / (1.0 + jnp.exp(-value))


def put_products(low, pd, sel, maps, rank, part_ref, rows):
    part_ref[rows, 0:rank] = jnp.dot(low, pd, preferred_element_type=F32).astype(BF16)
    both = lax.dot_general(low, sel, (((1,), (1,)), ((), ())), preferred_element_type=F32)
    high = both.astype(BF16).astype(F32)
    lane = lax.broadcasted_iota(jnp.int32, both.shape, 1)
    part_ref[rows, rank : rank + LANES] = jnp.where(lane < maps, high, both - high).astype(BF16)


def project_kernel(
    x_hbm, pd_hbm, ps_hbm, weight_hbm, bias_hbm, dw_hbm, log_hbm, dbias_hbm, gain_hbm,
    act_ref, part_ref, head_ref, pd_ref, sel_ref, taps_ref, dw_ref, rate_ref, vecs_ref,
    x_ref, log_ref, weight_ref, bias_ref, ps_ref, xs, xp, low, sems,
):
    rows, width = x_ref.shape
    steps = rows // CHUNKS
    rank = pd_ref.shape[1]
    maps = ps_ref.shape[0]
    halves = width // LANES
    pairs = (
        (x_hbm, x_ref), (weight_hbm, weight_ref), (bias_hbm, bias_ref), (ps_hbm, ps_ref), (pd_hbm, pd_ref),
        (log_hbm, log_ref), (dw_hbm, dw_ref), (dbias_hbm, vecs_ref.at[0:1]), (gain_hbm, vecs_ref.at[1:2]),
    )
    copies = [pltpu.make_async_copy(source, target, sems.at[i]) for i, (source, target) in enumerate(pairs)]
    for copy in copies:
        copy.start()
    copies[0].wait()
    head_ref[...] = x_ref[0:16, :].astype(F32)[0:8, :]
    for half in range(halves):
        cols = slice(half * LANES, (half + 1) * LANES)
        xs[half, 0:8, :] = jnp.zeros((8, LANES), F32)
        xs[half, 8 : 8 + rows, :] = x_ref[:, cols].astype(F32)
        for step in range(-(KWIDTH - 1), steps):
            to = (step + KWIDTH - 1) * CHUNKS
            xp[half, to : to + CHUNKS, :] = xs[half, pl.ds(8 + step, CHUNKS, stride=steps), :]
    copies[1].wait()
    copies[2].wait()
    taps_ref[0:KWIDTH, :] = weight_ref[...]
    taps_ref[KWIDTH : KWIDTH + 1, :] = bias_ref[...]
    block = min(rows, 64)
    for half in range(halves):
        cols = slice(half * LANES, (half + 1) * LANES)
        for start in range(0, rows, block):
            value = bias_ref[:, cols]
            for tap in range(KWIDTH):
                at = start + tap * CHUNKS
                value = value + weight_ref[tap : tap + 1, cols] * xp[half, at : at + block, :]
            value = silu(value)
            act_ref[start : start + block, cols] = value
            low[start : start + block, cols] = value.astype(BF16)
    copies[3].wait()
    sel_ref[...] = jnp.zeros_like(sel_ref)
    sel_ref[0:maps, :] = ps_ref[...]
    sel_ref[maps : 2 * maps, :] = ps_ref[...]
    copies[4].wait()
    put_products(low[...], pd_ref[...], sel_ref[...], maps, rank, part_ref, slice(0, rows))
    copies[5].wait()
    rate_ref[...] = -jnp.exp(log_ref[...]) * LOG2E
    for copy in copies[6:]:
        copy.wait()


def head_kernel(maps, halo_ref, head_ref, taps_ref, pd_ref, sel_ref, act_in, part_in, act_ref, part_ref, ext):
    rank = pd_ref.shape[1]
    ext[0:8, :] = halo_ref[...].astype(F32)[-8:, :]
    ext[8:16, :] = head_ref[...]
    value = taps_ref[KWIDTH : KWIDTH + 1, :]
    for tap in range(KWIDTH):
        at = 8 - (KWIDTH - 1) + tap
        value = value + taps_ref[tap : tap + 1, :] * ext[at : at + 8, :]
    value = silu(value)
    act_ref[...] = act_in[...]
    part_ref[...] = part_in[...]
    for token in range(KWIDTH - 1):
        act_ref[token * CHUNKS : token * CHUNKS + 1, :] = value[token : token + 1, :]
    low = act_ref[0:HEAD, :].astype(BF16)
    put_products(low, pd_ref[...], sel_ref[...], maps, rank, part_ref, slice(0, HEAD))


def total_kernel(rank, maps, parts_ref, out_ref):
    devices, rows, width = parts_ref.shape
    total = parts_ref[0].astype(F32)
    for source in range(1, devices):
        total = total + parts_ref[source].astype(F32)
    chosen = total[:, rank:]
    lane = lax.broadcasted_iota(jnp.int32, chosen.shape, 1)
    summed = chosen + pltpu.roll(chosen, LANES - maps, 1)
    twice = jnp.where(lane < maps, summed, pltpu.roll(summed, maps, 1))
    high = twice.astype(BF16).astype(F32)
    rest = jnp.where(lane < 2 * maps, twice - high, 0.0)
    mixed = jnp.where(lane < maps, high, rest)
    row = jnp.concatenate([total[:, :rank], mixed], axis=1).astype(BF16)
    for target in range(devices):
        out_ref[target] = row


def spread(first, maps):
    shape = (LANES, STATE * LANES)
    source = lax.broadcasted_iota(jnp.int32, shape, 0)
    group = lax.broadcasted_iota(jnp.int32, shape, 1) >> 7
    hit = (source == group + first) | (source == group + (first + maps))
    return jnp.where(hit, 1.0, 0.0).astype(BF16)


def step_rows(step):
    return pl.ds(pl.multiple_of(step * CHUNKS, CHUNKS), CHUNKS)


def ends_kernel(
    rank, me_ref, g_ref, act_ref, dw_ref, vecs_ref, rate,
    delta_hbm, inside_hbm, before_hbm, pay_hbm,
    delta, inside_ref, before_ref, pay_ref, drive, b_all, cum_ref, ends, sems,
):
    rows, width = act_ref.shape
    steps = rows // CHUNKS
    halves = width // LANES
    z = jnp.dot(g_ref[:, :rank], dw_ref[...], preferred_element_type=F32) + vecs_ref[0:1, :]
    step_size = jnp.maximum(z, 0.0) + jnp.log1p(jnp.exp(-jnp.abs(z)))
    delta[...] = step_size
    pairs = ((delta, delta_hbm), (inside_ref, inside_hbm), (before_ref, before_hbm), (pay_ref, pay_hbm))
    copies = [pltpu.make_async_copy(source, target, sems.at[i]) for i, (source, target) in enumerate(pairs)]
    copies[0].start()
    drive[...] = step_size * act_ref[...]
    b_all[...] = jnp.dot(g_ref[:, rank:], spread(0, 2 * STATE), preferred_element_type=F32)
    chunk = lax.broadcasted_iota(jnp.int32, (CHUNKS, LANES), 0)
    zero = jnp.zeros((CHUNKS, LANES), F32)

    def add(step, totals):
        at = step_rows(step)
        totals = [totals[half] + delta[at, half * LANES : (half + 1) * LANES] for half in range(halves)]
        for half in range(halves):
            cum_ref[at, half * LANES : (half + 1) * LANES] = totals[half]
        return totals

    totals = lax.fori_loop(0, steps, add, [zero] * halves, unroll=8)
    for half in range(halves):
        cols = slice(half * LANES, (half + 1) * LANES)
        rates = [jnp.broadcast_to(rate[n : n + 1, cols], (CHUNKS, LANES)) for n in range(STATE)]
        total = totals[half]

        def gather(step, states, cols=cols, rates=rates, total=total):
            at = step_rows(step)
            left = total - cum_ref[at, cols]
            push = drive[at, cols]
            return [
                states[n] + jnp.exp2(left * rates[n]) * (push * b_all[at, n * LANES : (n + 1) * LANES])
                for n in range(STATE)
            ]

        states = lax.fori_loop(0, steps, gather, [zero] * STATE, unroll=8)
        sums = [total]
        shift = 1
        while shift < CHUNKS:
            sums.append(sums[-1] + jnp.where(chunk >= shift, pltpu.roll(sums[-1], shift, 0), 0.0))
            shift *= 2
        for n in range(STATE):
            end = states[n]
            shift = 1
            for level in range(len(sums) - 1):
                end = end + jnp.exp2(rates[n] * sums[level]) * jnp.where(
                    chunk >= shift, pltpu.roll(end, shift, 0), 0.0
                )
                shift *= 2
            inside_ref[n, :, cols] = jnp.where(chunk >= 1, pltpu.roll(end, 1, 0), 0.0)
            ends[n : n + 1, cols] = end[CHUNKS - 1 :, :]
        before_ref[:, cols] = jnp.where(chunk >= 1, pltpu.roll(sums[-1], 1, 0), 0.0)
        ends[STATE : STATE + 1, cols] = sums[-1][CHUNKS - 1 :, :]

    copies[1].start()
    copies[2].start()
    me = me_ref[0]
    value = ends[0:STATE, :]
    total = jnp.broadcast_to(ends[STATE : STATE + 1, :], value.shape)
    high = total.astype(BF16).astype(F32)
    first = lax.broadcasted_iota(jnp.int32, value.shape, 0) == 0
    tail = jnp.where(first, high, total - high)
    for target in range(pay_ref.shape[0]):
        use = target > me
        pay_ref[target, 0:16, :] = jnp.where(use, value, 0.0).astype(BF16)
        pay_ref[target, 16:32, :] = jnp.where(use, tail, 0.0).astype(BF16)
    copies[3].start()
    for copy in copies:
        copy.wait()


def local_kernel(
    rank, g_ref, act_ref, rate, vecs_ref, delta_hbm, inside_hbm, before_hbm, gate_hbm,
    y_ref, cum_ref, lit_ref, spread_ref, maps_ref,
    b_all, c_all, delta, inside_ref, before_ref, gate_ref, sems,
):
    rows, width = act_ref.shape
    steps = rows // CHUNKS
    halves = width // LANES
    pairs = ((delta_hbm, delta), (inside_hbm, inside_ref), (before_hbm, before_ref), (gate_hbm, gate_ref))
    copies = [pltpu.make_async_copy(source, target, sems.at[i]) for i, (source, target) in enumerate(pairs)]
    for copy in copies:
        copy.start()
    b_all[...] = jnp.dot(g_ref[:, rank:], spread(0, 2 * STATE), preferred_element_type=F32)
    spread_ref[...] = spread(STATE, 2 * STATE)
    maps_ref[...] = g_ref[:, rank:]
    c_all[...] = jnp.dot(maps_ref[...], spread_ref[...], preferred_element_type=F32)
    for copy in copies:
        copy.wait()
    for half in range(halves):
        cols = slice(half * LANES, (half + 1) * LANES)
        rates = [jnp.broadcast_to(rate[n : n + 1, cols], (CHUNKS, LANES)) for n in range(STATE)]
        gain = vecs_ref[1:2, cols]

        def advance(step, carried, cols=cols, rates=rates, gain=gain):
            states, total = carried
            at = step_rows(step)
            size = delta[at, cols]
            value = act_ref[at, cols]
            push = size * value
            total = total + size
            out = gain * value
            later = []
            for n in range(STATE):
                group = slice(n * LANES, (n + 1) * LANES)
                now = jnp.exp2(size * rates[n]) * states[n] + push * b_all[at, group]
                out = out + c_all[at, group] * now
                later.append(now)
            y_ref[at, cols] = out
            cum_ref[at, cols] = total
            return later, total

        lax.fori_loop(
            0, steps, advance, ([inside_ref[n, :, cols] for n in range(STATE)], before_ref[:, cols]), unroll=4
        )
    lit_ref[...] = silu(gate_ref[...].astype(F32))


def finish_kernel(got_ref, maps_ref, spread_ref, y_ref, cum_ref, rate, lit_ref, out_ref, c_all, carry, ys):
    rows, width = y_ref.shape
    steps = rows // CHUNKS
    halves = width // LANES
    c_all[...] = jnp.dot(maps_ref[...], spread_ref[...], preferred_element_type=F32)
    incoming = jnp.zeros((STATE, width), F32)
    for source in range(got_ref.shape[0] - 1):
        tail = got_ref[source, 16:32, :].astype(F32)
        decay = jnp.exp2(rate[...] * (tail[0:1, :] + tail[1:2, :]))
        incoming = decay * incoming + got_ref[source, 0:16, :].astype(F32)
    carry[...] = incoming
    for half in range(halves):
        cols = slice(half * LANES, (half + 1) * LANES)
        rates = [jnp.broadcast_to(rate[n : n + 1, cols], (CHUNKS, LANES)) for n in range(STATE)]
        entering = [jnp.broadcast_to(carry[n : n + 1, cols], (CHUNKS, LANES)) for n in range(STATE)]

        def correct(step, _, half=half, cols=cols, rates=rates, entering=entering):
            at = step_rows(step)
            total = cum_ref[at, cols]
            out = y_ref[at, cols]
            for n in range(STATE):
                group = slice(n * LANES, (n + 1) * LANES)
                out = out + (c_all[at, group] * entering[n]) * jnp.exp2(total * rates[n])
            ys[half, pl.ds(step, CHUNKS, stride=steps), :] = out
            return 0

        lax.fori_loop(0, steps, correct, 0, unroll=8)
        out_ref[:, cols] = (ys[half] * lit_ref[:, cols]).astype(BF16)


def on_device(
    mamba_in, mamba_gate, conv_weight, conv_bias, proj_delta, proj_select, delta_weight, delta_bias, decay_log, skip_gain,
):
    rows, width = mamba_in.shape
    rank = proj_delta.shape[1]
    maps = proj_select.shape[1]
    halves = width // LANES
    steps = rows // CHUNKS
    n_ctx, n_ch = lax.axis_size("ctx"), lax.axis_size("ch")
    wide = rank + LANES
    me = lax.axis_index("ctx").astype(jnp.int32).reshape(1)
    cells = rows * width * STATE
    tile = jax.ShapeDtypeStruct((rows, width), F32)
    part_shape = jax.ShapeDtypeStruct((rows, wide), BF16)
    big = pltpu.VMEM((rows, STATE * LANES), F32)

    halo = lax.ppermute(mamba_in[rows - 16 :], "ctx", [(i, i + 1) for i in range(n_ctx - 1)])
    act, part, head, pd, sel, taps, dw, rate, vecs = pl.pallas_call(
        project_kernel,
        out_shape=(
            tile,
            part_shape,
            jax.ShapeDtypeStruct((8, width), F32),
            jax.ShapeDtypeStruct(proj_delta.shape, BF16),
            jax.ShapeDtypeStruct((LANES, width), BF16),
            jax.ShapeDtypeStruct((8, width), F32),
            jax.ShapeDtypeStruct(delta_weight.shape, BF16),
            jax.ShapeDtypeStruct((STATE, width), F32),
            jax.ShapeDtypeStruct((8, width), F32),
        ),
        in_specs=hbm(9),
        out_specs=tuple(vmem(9)),
        scratch_shapes=[
            pltpu.VMEM((rows, width), BF16),
            pltpu.VMEM((STATE, width), F32),
            pltpu.VMEM((KWIDTH, width), F32),
            pltpu.VMEM((1, width), F32),
            pltpu.VMEM((maps, width), BF16),
            pltpu.VMEM((halves, rows + 8, LANES), F32),
            pltpu.VMEM((halves, (steps + KWIDTH - 1) * CHUNKS, LANES), F32),
            pltpu.VMEM((rows, width), BF16),
            pltpu.SemaphoreType.DMA((9,)),
        ],
        compiler_params=pltpu.CompilerParams(vmem_limit_bytes=16 * MIB),
        cost_estimate=pl.CostEstimate(
            flops=2 * rows * width * wide, bytes_accessed=2 * rows * width * 8, transcendentals=rows * width
        ),
        name="project",
    )(
        *stay(
            mamba_in, proj_delta, proj_select.T, conv_weight, conv_bias[None, :],
            delta_weight, decay_log, delta_bias[None, :], skip_gain[None, :],
        )
    )
    act, part = pl.pallas_call(
        functools.partial(head_kernel, maps),
        out_shape=(tile, part_shape),
        in_specs=vmem(7),
        out_specs=tuple(vmem(2)),
        scratch_shapes=[pltpu.VMEM((16, width), F32)],
        compiler_params=pltpu.CompilerParams(vmem_limit_bytes=16 * MIB),
        name="first_rows",
    )(halo, head, taps, pd, sel, act, part)

    parts = lax.all_to_all(part.reshape(n_ch, rows // n_ch, wide), "ch", 0, 0)
    totals = pl.pallas_call(
        functools.partial(total_kernel, rank, maps),
        out_shape=jax.ShapeDtypeStruct(parts.shape, BF16),
        in_specs=vmem(1),
        out_specs=vmem(1)[0],
        compiler_params=pltpu.CompilerParams(vmem_limit_bytes=16 * MIB),
        name="total",
    )(parts)
    gathered = lax.all_to_all(totals, "ch", 0, 0).reshape(rows, wide)

    sent = (
        ((rows, width), F32),
        ((STATE, CHUNKS, width), F32),
        ((CHUNKS, width), F32),
        ((n_ctx, 2 * STATE, width), BF16),
    )
    delta, inside, before, pay = pl.pallas_call(
        functools.partial(ends_kernel, rank),
        out_shape=tuple(pltpu.HBM(*kept) for kept in sent),
        in_specs=[pl.BlockSpec(memory_space=pltpu.SMEM)] + vmem(5),
        out_specs=tuple(hbm(4)),
        scratch_shapes=[
            *(pltpu.VMEM(*kept) for kept in sent),
            pltpu.VMEM((rows, width), F32),
            big,
            pltpu.VMEM((rows, width), F32),
            pltpu.VMEM((STATE + 8, width), F32),
            pltpu.SemaphoreType.DMA((4,)),
        ],
        compiler_params=pltpu.CompilerParams(vmem_limit_bytes=16 * MIB),
        name="ends",
    )(me, gathered, act, dw, vecs, rate)

    got = lax.all_to_all(pay, "ctx", 0, 0)
    y_local, cum, lit, spread_c, maps_all = pl.pallas_call(
        functools.partial(local_kernel, rank),
        out_shape=(
            tile,
            tile,
            tile,
            jax.ShapeDtypeStruct((LANES, STATE * LANES), BF16),
            jax.ShapeDtypeStruct((rows, LANES), BF16),
        ),
        in_specs=vmem(4) + hbm(4),
        out_specs=tuple(vmem(5)),
        scratch_shapes=[
            big,
            big,
            *(pltpu.VMEM(*kept) for kept in sent[:3]),
            pltpu.VMEM((rows, width), BF16),
            pltpu.SemaphoreType.DMA((4,)),
        ],
        compiler_params=pltpu.CompilerParams(vmem_limit_bytes=24 * MIB),
        cost_estimate=pl.CostEstimate(flops=6 * cells, bytes_accessed=8 * rows * width * 4, transcendentals=cells),
        name="local_scan",
    )(gathered, act, rate, vecs, *stay(delta, inside, before, mamba_gate))
    return pl.pallas_call(
        finish_kernel,
        out_shape=jax.ShapeDtypeStruct((rows, width), BF16),
        in_specs=vmem(7),
        out_specs=vmem(1)[0],
        scratch_shapes=[
            big,
            pltpu.VMEM((STATE, width), F32),
            pltpu.VMEM((halves, rows, LANES), F32),
        ],
        compiler_params=pltpu.CompilerParams(vmem_limit_bytes=16 * MIB),
        name="finish",
    )(got, maps_all, spread_c, y_local, cum, rate, lit)


def solution(mesh):
    return jax.shard_map(
        on_device,
        mesh=mesh,
        in_specs=(
            P("ctx", "ch"),
            P("ctx", "ch"),
            P(None, "ch"),
            P("ch"),
            P("ch", None),
            P("ch", None),
            P(None, "ch"),
            P("ch"),
            P(None, "ch"),
            P("ch"),
        ),
        out_specs=P("ctx", "ch"),
        check_vma=False,
    )
```

```python
import functools
import math

import jax
import jax.numpy as jnp
from jax import lax
from jax.experimental import pallas as pl
from jax.experimental.pallas import tpu as pltpu
from jax.sharding import PartitionSpec as P

STATE = 16
KWIDTH = 4
LANES = 128
CHUNKS = 8
HEAD = 32
LOG2E = 1.0 / math.log(2.0)
MIB = 1 << 20
F32 = jnp.float32
BF16 = jnp.bfloat16


def vmem(count):
    return [pl.BlockSpec(memory_space=pltpu.VMEM)] * count


def hbm(count):
    return [pl.BlockSpec(memory_space=pltpu.HBM)] * count


def stay(*arrays):
    return [pltpu.with_memory_space_constraint(array, pltpu.HBM) for array in arrays]


def silu(value):
    return value / (1.0 + jnp.exp(-value))


def put_products(low, pd, sel, maps, rank, part_ref, rows):
    part_ref[rows, 0:rank] = jnp.dot(low, pd, preferred_element_type=F32).astype(BF16)
    both = lax.dot_general(low, sel, (((1,), (1,)), ((), ())), preferred_element_type=F32)
    high = both.astype(BF16).astype(F32)
    lane = lax.broadcasted_iota(jnp.int32, both.shape, 1)
    part_ref[rows, rank : rank + LANES] = jnp.where(lane < maps, high, both - high).astype(BF16)


def project_kernel(
    x_hbm, pd_hbm, ps_hbm, weight_hbm, bias_hbm, dw_hbm, log_hbm, dbias_hbm, gain_hbm,
    act_ref, part_ref, head_ref, pd_ref, sel_ref, taps_ref, dw_ref, rate_ref, vecs_ref,
    x_ref, log_ref, weight_ref, bias_ref, ps_ref, xs, xp, low, sems,
):
    rows, width = x_ref.shape
    steps = rows // CHUNKS
    rank = pd_ref.shape[1]
    maps = ps_ref.shape[0]
    halves = width // LANES
    pairs = (
        (x_hbm, x_ref), (weight_hbm, weight_ref), (bias_hbm, bias_ref), (ps_hbm, ps_ref), (pd_hbm, pd_ref),
        (log_hbm, log_ref), (dw_hbm, dw_ref), (dbias_hbm, vecs_ref.at[0:1]), (gain_hbm, vecs_ref.at[1:2]),
    )
    copies = [pltpu.make_async_copy(source, target, sems.at[i]) for i, (source, target) in enumerate(pairs)]
    for copy in copies:
        copy.start()
    copies[0].wait()
    head_ref[...] = x_ref[0:16, :].astype(F32)[0:8, :]
    for half in range(halves):
        cols = slice(half * LANES, (half + 1) * LANES)
        xs[half, 0:8, :] = jnp.zeros((8, LANES), F32)
        xs[half, 8 : 8 + rows, :] = x_ref[:, cols].astype(F32)
        for step in range(-(KWIDTH - 1), steps):
            to = (step + KWIDTH - 1) * CHUNKS
            xp[half, to : to + CHUNKS, :] = xs[half, pl.ds(8 + step, CHUNKS, stride=steps), :]
    copies[1].wait()
    copies[2].wait()
    taps_ref[0:KWIDTH, :] = weight_ref[...]
    taps_ref[KWIDTH : KWIDTH + 1, :] = bias_ref[...]
    block = min(rows, 64)
    for half in range(halves):
        cols = slice(half * LANES, (half + 1) * LANES)
        for start in range(0, rows, block):
            value = bias_ref[:, cols]
            for tap in range(KWIDTH):
                at = start + tap * CHUNKS
                value = value + weight_ref[tap : tap + 1, cols] * xp[half, at : at + block, :]
            value = silu(value)
            act_ref[start : start + block, cols] = value
            low[start : start + block, cols] = value.astype(BF16)
    copies[3].wait()
    sel_ref[...] = jnp.zeros_like(sel_ref)
    sel_ref[0:maps, :] = ps_ref[...]
    sel_ref[maps : 2 * maps, :] = ps_ref[...]
    copies[4].wait()
    put_products(low[...], pd_ref[...], sel_ref[...], maps, rank, part_ref, slice(0, rows))
    copies[5].wait()
    rate_ref[...] = -jnp.exp(log_ref[...]) * LOG2E
    for copy in copies[6:]:
        copy.wait()


def head_kernel(maps, halo_ref, head_ref, taps_ref, pd_ref, sel_ref, act_in, part_in, act_ref, part_ref, ext):
    rank = pd_ref.shape[1]
    ext[0:8, :] = halo_ref[...].astype(F32)[-8:, :]
    ext[8:16, :] = head_ref[...]
    value = taps_ref[KWIDTH : KWIDTH + 1, :]
    for tap in range(KWIDTH):
        at = 8 - (KWIDTH - 1) + tap
        value = value + taps_ref[tap : tap + 1, :] * ext[at : at + 8, :]
    value = silu(value)
    act_ref[...] = act_in[...]
    part_ref[...] = part_in[...]
    for token in range(KWIDTH - 1):
        act_ref[token * CHUNKS : token * CHUNKS + 1, :] = value[token : token + 1, :]
    low = act_ref[0:HEAD, :].astype(BF16)
    put_products(low, pd_ref[...], sel_ref[...], maps, rank, part_ref, slice(0, HEAD))


def total_kernel(rank, maps, parts_ref, out_ref):
    devices, rows, width = parts_ref.shape
    total = parts_ref[0].astype(F32)
    for source in range(1, devices):
        total = total + parts_ref[source].astype(F32)
    chosen = total[:, rank:]
    lane = lax.broadcasted_iota(jnp.int32, chosen.shape, 1)
    summed = chosen + pltpu.roll(chosen, LANES - maps, 1)
    twice = jnp.where(lane < maps, summed, pltpu.roll(summed, maps, 1))
    high = twice.astype(BF16).astype(F32)
    rest = jnp.where(lane < 2 * maps, twice - high, 0.0)
    mixed = jnp.where(lane < maps, high, rest)
    row = jnp.concatenate([total[:, :rank], mixed], axis=1).astype(BF16)
    for target in range(devices):
        out_ref[target] = row


def ready_kernel(gate_ref, lit_ref, spread_ref):
    lit_ref[...] = silu(gate_ref[...].astype(F32))
    source = lax.broadcasted_iota(jnp.int32, spread_ref.shape, 0)
    group = lax.broadcasted_iota(jnp.int32, spread_ref.shape, 1) >> 7
    hit = (source == group) | (source == group + 2 * STATE)
    spread_ref[...] = jnp.where(hit, 1.0, 0.0).astype(BF16)


def step_rows(step):
    return pl.ds(pl.multiple_of(step * CHUNKS, CHUNKS), CHUNKS)


def ends_kernel(
    rank, me_ref, g_ref, act_ref, dw_ref, vecs_ref, rate, spread_ref,
    delta_hbm, inside_hbm, before_hbm, pay_hbm,
    delta, inside_ref, before_ref, pay_ref, drive, b_all, cum_ref, ends, sems,
):
    rows, width = act_ref.shape
    steps = rows // CHUNKS
    halves = width // LANES
    z = jnp.dot(g_ref[:, :rank], dw_ref[...], preferred_element_type=F32) + vecs_ref[0:1, :]
    step_size = jnp.maximum(z, 0.0) + jnp.log1p(jnp.exp(-jnp.abs(z)))
    delta[...] = step_size
    pairs = ((delta, delta_hbm), (inside_ref, inside_hbm), (before_ref, before_hbm), (pay_ref, pay_hbm))
    copies = [pltpu.make_async_copy(source, target, sems.at[i]) for i, (source, target) in enumerate(pairs)]
    copies[0].start()
    drive[...] = step_size * act_ref[...]
    b_all[...] = jnp.dot(g_ref[:, rank:], spread_ref[...], preferred_element_type=F32)
    chunk = lax.broadcasted_iota(jnp.int32, (CHUNKS, LANES), 0)
    zero = jnp.zeros((CHUNKS, LANES), F32)

    def add(step, totals):
        at = step_rows(step)
        totals = [totals[half] + delta[at, half * LANES : (half + 1) * LANES] for half in range(halves)]
        for half in range(halves):
            cum_ref[at, half * LANES : (half + 1) * LANES] = totals[half]
        return totals

    totals = lax.fori_loop(0, steps, add, [zero] * halves, unroll=8)
    for half in range(halves):
        cols = slice(half * LANES, (half + 1) * LANES)
        rates = [jnp.broadcast_to(rate[n : n + 1, cols], (CHUNKS, LANES)) for n in range(STATE)]
        total = totals[half]

        def gather(step, states, cols=cols, rates=rates, total=total):
            at = step_rows(step)
            left = total - cum_ref[at, cols]
            push = drive[at, cols]
            return [
                states[n] + jnp.exp2(left * rates[n]) * (push * b_all[at, n * LANES : (n + 1) * LANES])
                for n in range(STATE)
            ]

        states = lax.fori_loop(0, steps, gather, [zero] * STATE, unroll=8)
        sums = [total]
        shift = 1
        while shift < CHUNKS:
            sums.append(sums[-1] + jnp.where(chunk >= shift, pltpu.roll(sums[-1], shift, 0), 0.0))
            shift *= 2
        for n in range(STATE):
            end = states[n]
            shift = 1
            for level in range(len(sums) - 1):
                end = end + jnp.exp2(rates[n] * sums[level]) * jnp.where(
                    chunk >= shift, pltpu.roll(end, shift, 0), 0.0
                )
                shift *= 2
            inside_ref[n, :, cols] = jnp.where(chunk >= 1, pltpu.roll(end, 1, 0), 0.0)
            ends[n : n + 1, cols] = end[CHUNKS - 1 :, :]
        before_ref[:, cols] = jnp.where(chunk >= 1, pltpu.roll(sums[-1], 1, 0), 0.0)
        ends[STATE : STATE + 1, cols] = sums[-1][CHUNKS - 1 :, :]

    copies[1].start()
    copies[2].start()
    me = me_ref[0]
    value = ends[0:STATE, :]
    total = jnp.broadcast_to(ends[STATE : STATE + 1, :], value.shape)
    high = total.astype(BF16).astype(F32)
    first = lax.broadcasted_iota(jnp.int32, value.shape, 0) == 0
    tail = jnp.where(first, high, total - high)
    for target in range(pay_ref.shape[0]):
        use = target > me
        pay_ref[target, 0:16, :] = jnp.where(use, value, 0.0).astype(BF16)
        pay_ref[target, 16:32, :] = jnp.where(use, tail, 0.0).astype(BF16)
    copies[3].start()
    for copy in copies:
        copy.wait()


def finish_kernel(
    rank, got_ref, g_ref, act_ref, rate, vecs_ref, lit_ref, spread_ref, delta_hbm, inside_hbm, before_hbm,
    out_hbm,
    delta, inside_ref, before_ref, b_all, c_all, carry, ys, out_ref, sems,
):
    rows, width = act_ref.shape
    steps = rows // CHUNKS
    halves = width // LANES
    pairs = ((delta_hbm, delta), (inside_hbm, inside_ref), (before_hbm, before_ref))
    copies = [pltpu.make_async_copy(source, target, sems.at[i]) for i, (source, target) in enumerate(pairs)]
    for copy in copies:
        copy.start()
    maps = g_ref[:, rank:]
    b_all[...] = jnp.dot(maps, spread_ref[...], preferred_element_type=F32)
    maps = pltpu.roll(maps.astype(F32), LANES - STATE, 1).astype(BF16)
    c_all[...] = jnp.dot(maps, spread_ref[...], preferred_element_type=F32)
    incoming = jnp.zeros((STATE, width), F32)
    for source in range(got_ref.shape[0] - 1):
        tail = got_ref[source, 16:32, :].astype(F32)
        decay = jnp.exp2(rate[...] * (tail[0:1, :] + tail[1:2, :]))
        incoming = decay * incoming + got_ref[source, 0:16, :].astype(F32)
    carry[...] = incoming
    for copy in copies:
        copy.wait()
    leaving = []
    for half in range(halves):
        cols = slice(half * LANES, (half + 1) * LANES)
        rates = [jnp.broadcast_to(rate[n : n + 1, cols], (CHUNKS, LANES)) for n in range(STATE)]
        gain = vecs_ref[1:2, cols]
        before = before_ref[:, cols]
        entering = [
            inside_ref[n, :, cols] + jnp.exp2(rates[n] * before) * carry[n : n + 1, cols] for n in range(STATE)
        ]

        def advance(step, states, half=half, cols=cols, rates=rates, gain=gain):
            at = step_rows(step)
            size = delta[at, cols]
            value = act_ref[at, cols]
            push = size * value
            out = gain * value
            later = []
            for n in range(STATE):
                group = slice(n * LANES, (n + 1) * LANES)
                now = jnp.exp2(size * rates[n]) * states[n] + push * b_all[at, group]
                out = out + c_all[at, group] * now
                later.append(now)
            ys[half, pl.ds(step, CHUNKS, stride=steps), :] = out
            return later

        lax.fori_loop(0, steps, advance, entering, unroll=8)
        out_ref[half] = (ys[half] * lit_ref[:, cols]).astype(BF16)
        copy = pltpu.make_async_copy(out_ref.at[half], out_hbm.at[:, cols], sems.at[len(pairs) + half])
        copy.start()
        leaving.append(copy)
    for copy in leaving:
        copy.wait()


def on_device(
    mamba_in, mamba_gate, conv_weight, conv_bias, proj_delta, proj_select, delta_weight, delta_bias, decay_log, skip_gain,
):
    rows, width = mamba_in.shape
    rank = proj_delta.shape[1]
    maps = proj_select.shape[1]
    halves = width // LANES
    steps = rows // CHUNKS
    n_ctx, n_ch = lax.axis_size("ctx"), lax.axis_size("ch")
    wide = rank + LANES
    me = lax.axis_index("ctx").astype(jnp.int32).reshape(1)
    tile = jax.ShapeDtypeStruct((rows, width), F32)
    part_shape = jax.ShapeDtypeStruct((rows, wide), BF16)
    big = pltpu.VMEM((rows, STATE * LANES), F32)

    halo = lax.ppermute(mamba_in[rows - 16 :], "ctx", [(i, i + 1) for i in range(n_ctx - 1)])
    act, part, head, pd, sel, taps, dw, rate, vecs = pl.pallas_call(
        project_kernel,
        out_shape=(
            tile,
            part_shape,
            jax.ShapeDtypeStruct((8, width), F32),
            jax.ShapeDtypeStruct(proj_delta.shape, BF16),
            jax.ShapeDtypeStruct((LANES, width), BF16),
            jax.ShapeDtypeStruct((8, width), F32),
            jax.ShapeDtypeStruct(delta_weight.shape, BF16),
            jax.ShapeDtypeStruct((STATE, width), F32),
            jax.ShapeDtypeStruct((8, width), F32),
        ),
        in_specs=hbm(9),
        out_specs=tuple(vmem(9)),
        scratch_shapes=[
            pltpu.VMEM((rows, width), BF16),
            pltpu.VMEM((STATE, width), F32),
            pltpu.VMEM((KWIDTH, width), F32),
            pltpu.VMEM((1, width), F32),
            pltpu.VMEM((maps, width), BF16),
            pltpu.VMEM((halves, rows + 8, LANES), F32),
            pltpu.VMEM((halves, (steps + KWIDTH - 1) * CHUNKS, LANES), F32),
            pltpu.VMEM((rows, width), BF16),
            pltpu.SemaphoreType.DMA((9,)),
        ],
        compiler_params=pltpu.CompilerParams(vmem_limit_bytes=16 * MIB),
        cost_estimate=pl.CostEstimate(
            flops=2 * rows * width * wide, bytes_accessed=2 * rows * width * 8, transcendentals=rows * width
        ),
        name="project",
    )(
        *stay(
            mamba_in, proj_delta, proj_select.T, conv_weight, conv_bias[None, :],
            delta_weight, decay_log, delta_bias[None, :], skip_gain[None, :],
        )
    )
    act, part = pl.pallas_call(
        functools.partial(head_kernel, maps),
        out_shape=(tile, part_shape),
        in_specs=vmem(7),
        out_specs=tuple(vmem(2)),
        scratch_shapes=[pltpu.VMEM((16, width), F32)],
        compiler_params=pltpu.CompilerParams(vmem_limit_bytes=16 * MIB),
        name="first_rows",
    )(halo, head, taps, pd, sel, act, part)

    lit, spread = pl.pallas_call(
        ready_kernel,
        out_shape=(tile, jax.ShapeDtypeStruct((LANES, STATE * LANES), BF16)),
        in_specs=vmem(1),
        out_specs=tuple(vmem(2)),
        compiler_params=pltpu.CompilerParams(vmem_limit_bytes=16 * MIB),
        cost_estimate=pl.CostEstimate(
            flops=16 * rows * width, bytes_accessed=8 * rows * width, transcendentals=rows * width
        ),
        name="ready",
    )(mamba_gate)
    parts = lax.all_to_all(part.reshape(n_ch, rows // n_ch, wide), "ch", 0, 0)
    totals = pl.pallas_call(
        functools.partial(total_kernel, rank, maps),
        out_shape=jax.ShapeDtypeStruct(parts.shape, BF16),
        in_specs=vmem(1),
        out_specs=vmem(1)[0],
        compiler_params=pltpu.CompilerParams(vmem_limit_bytes=16 * MIB),
        name="total",
    )(parts)
    gathered = lax.all_to_all(totals, "ch", 0, 0).reshape(rows, wide)

    sent = (
        ((rows, width), F32),
        ((STATE, CHUNKS, width), F32),
        ((CHUNKS, width), F32),
        ((n_ctx, 2 * STATE, width), BF16),
    )
    delta, inside, before, pay = pl.pallas_call(
        functools.partial(ends_kernel, rank),
        out_shape=tuple(pltpu.HBM(*kept) for kept in sent),
        in_specs=[pl.BlockSpec(memory_space=pltpu.SMEM)] + vmem(6),
        out_specs=tuple(hbm(4)),
        scratch_shapes=[
            *(pltpu.VMEM(*kept) for kept in sent),
            pltpu.VMEM((rows, width), F32),
            big,
            pltpu.VMEM((rows, width), F32),
            pltpu.VMEM((STATE + 8, width), F32),
            pltpu.SemaphoreType.DMA((4,)),
        ],
        compiler_params=pltpu.CompilerParams(vmem_limit_bytes=16 * MIB),
        name="ends",
    )(me, gathered, act, dw, vecs, rate, spread)

    got = lax.all_to_all(pay, "ctx", 0, 0)
    return pl.pallas_call(
        functools.partial(finish_kernel, rank),
        out_shape=jax.ShapeDtypeStruct((rows, width), BF16),
        in_specs=vmem(7) + hbm(3),
        out_specs=hbm(1)[0],
        scratch_shapes=[
            *(pltpu.VMEM(*kept) for kept in sent[:3]),
            big,
            big,
            pltpu.VMEM((STATE, width), F32),
            pltpu.VMEM((halves, rows, LANES), F32),
            pltpu.VMEM((halves, rows, LANES), BF16),
            pltpu.SemaphoreType.DMA((3 + halves,)),
        ],
        compiler_params=pltpu.CompilerParams(vmem_limit_bytes=24 * MIB),
        name="finish",
    )(got, gathered, act, rate, vecs, lit, spread, *stay(delta, inside, before))


def solution(mesh):
    return jax.shard_map(
        on_device,
        mesh=mesh,
        in_specs=(
            P("ctx", "ch"),
            P("ctx", "ch"),
            P(None, "ch"),
            P("ch"),
            P("ch", None),
            P("ch", None),
            P(None, "ch"),
            P("ch"),
            P(None, "ch"),
            P("ch"),
        ),
        out_specs=P("ctx", "ch"),
        check_vma=False,
    )
```

```python
import functools
import math

import jax
import jax.numpy as jnp
from jax import lax
from jax.experimental import pallas as pl
from jax.experimental.pallas import tpu as pltpu
from jax.sharding import PartitionSpec as P

STATE = 16
KWIDTH = 4
LANES = 128
CHUNKS = 8
HEAD = 32
LOG2E = 1.0 / math.log(2.0)
MIB = 1 << 20
F32 = jnp.float32
BF16 = jnp.bfloat16


def vmem(count):
    return [pl.BlockSpec(memory_space=pltpu.VMEM)] * count


def hbm(count):
    return [pl.BlockSpec(memory_space=pltpu.HBM)] * count


def stay(*arrays):
    return [pltpu.with_memory_space_constraint(array, pltpu.HBM) for array in arrays]


def silu(value):
    return value / (1.0 + jnp.exp(-value))


def put_products(low, pd, sel, maps, rank, part_ref, rows):
    part_ref[rows, 0:rank] = jnp.dot(low, pd, preferred_element_type=F32).astype(BF16)
    both = lax.dot_general(low, sel, (((1,), (1,)), ((), ())), preferred_element_type=F32)
    high = both.astype(BF16).astype(F32)
    lane = lax.broadcasted_iota(jnp.int32, both.shape, 1)
    part_ref[rows, rank : rank + LANES] = jnp.where(lane < maps, high, both - high).astype(BF16)


def project_kernel(
    x_hbm, pd_hbm, ps_hbm, weight_hbm, bias_hbm, dw_hbm, log_hbm, dbias_hbm, gain_hbm,
    act_ref, part_ref, head_ref, pd_ref, sel_ref, taps_ref, dw_ref, rate_ref, vecs_ref,
    x_ref, log_ref, weight_ref, bias_ref, ps_ref, xs, xp, low, sems,
):
    rows, width = x_ref.shape
    steps = rows // CHUNKS
    rank = pd_ref.shape[1]
    maps = ps_ref.shape[0]
    halves = width // LANES
    pairs = (
        (x_hbm, x_ref), (weight_hbm, weight_ref), (bias_hbm, bias_ref), (ps_hbm, ps_ref), (pd_hbm, pd_ref),
        (log_hbm, log_ref), (dw_hbm, dw_ref), (dbias_hbm, vecs_ref.at[0:1]), (gain_hbm, vecs_ref.at[1:2]),
    )
    copies = [pltpu.make_async_copy(source, target, sems.at[i]) for i, (source, target) in enumerate(pairs)]
    for copy in copies:
        copy.start()
    copies[0].wait()
    head_ref[...] = x_ref[0:16, :].astype(F32)[0:8, :]
    for half in range(halves):
        cols = slice(half * LANES, (half + 1) * LANES)
        xs[half, 0:8, :] = jnp.zeros((8, LANES), F32)
        xs[half, 8 : 8 + rows, :] = x_ref[:, cols].astype(F32)
        for step in range(-(KWIDTH - 1), steps):
            to = (step + KWIDTH - 1) * CHUNKS
            xp[half, to : to + CHUNKS, :] = xs[half, pl.ds(8 + step, CHUNKS, stride=steps), :]
    copies[1].wait()
    copies[2].wait()
    taps_ref[0:KWIDTH, :] = weight_ref[...]
    taps_ref[KWIDTH : KWIDTH + 1, :] = bias_ref[...]
    block = min(rows, 64)
    for half in range(halves):
        cols = slice(half * LANES, (half + 1) * LANES)
        for start in range(0, rows, block):
            value = bias_ref[:, cols]
            for tap in range(KWIDTH):
                at = start + tap * CHUNKS
                value = value + weight_ref[tap : tap + 1, cols] * xp[half, at : at + block, :]
            value = silu(value)
            act_ref[start : start + block, cols] = value
            low[start : start + block, cols] = value.astype(BF16)
    copies[3].wait()
    sel_ref[...] = jnp.zeros_like(sel_ref)
    sel_ref[0:maps, :] = ps_ref[...]
    sel_ref[maps : 2 * maps, :] = ps_ref[...]
    copies[4].wait()
    put_products(low[...], pd_ref[...], sel_ref[...], maps, rank, part_ref, slice(0, rows))
    copies[5].wait()
    rate_ref[...] = -jnp.exp(log_ref[...]) * LOG2E
    for copy in copies[6:]:
        copy.wait()


def head_kernel(maps, halo_ref, head_ref, taps_ref, pd_ref, sel_ref, act_in, part_in, act_ref, part_ref, ext):
    rank = pd_ref.shape[1]
    ext[0:8, :] = halo_ref[...].astype(F32)[-8:, :]
    ext[8:16, :] = head_ref[...]
    value = taps_ref[KWIDTH : KWIDTH + 1, :]
    for tap in range(KWIDTH):
        at = 8 - (KWIDTH - 1) + tap
        value = value + taps_ref[tap : tap + 1, :] * ext[at : at + 8, :]
    value = silu(value)
    act_ref[...] = act_in[...]
    part_ref[...] = part_in[...]
    for token in range(KWIDTH - 1):
        act_ref[token * CHUNKS : token * CHUNKS + 1, :] = value[token : token + 1, :]
    low = act_ref[0:HEAD, :].astype(BF16)
    put_products(low, pd_ref[...], sel_ref[...], maps, rank, part_ref, slice(0, HEAD))


def total_kernel(rank, maps, parts_ref, out_ref):
    devices, rows, width = parts_ref.shape
    total = parts_ref[0].astype(F32)
    for source in range(1, devices):
        total = total + parts_ref[source].astype(F32)
    chosen = total[:, rank:]
    lane = lax.broadcasted_iota(jnp.int32, chosen.shape, 1)
    summed = chosen + pltpu.roll(chosen, LANES - maps, 1)
    twice = jnp.where(lane < maps, summed, pltpu.roll(summed, maps, 1))
    high = twice.astype(BF16).astype(F32)
    rest = jnp.where(lane < 2 * maps, twice - high, 0.0)
    mixed = jnp.where(lane < maps, high, rest)
    row = jnp.concatenate([total[:, :rank], mixed], axis=1).astype(BF16)
    for target in range(devices):
        out_ref[target] = row


def spread(first, maps):
    shape = (LANES, STATE * LANES)
    source = lax.broadcasted_iota(jnp.int32, shape, 0)
    group = lax.broadcasted_iota(jnp.int32, shape, 1) >> 7
    hit = (source == group + first) | (source == group + (first + maps))
    return jnp.where(hit, 1.0, 0.0).astype(BF16)


def step_rows(step):
    return pl.ds(pl.multiple_of(step * CHUNKS, CHUNKS), CHUNKS)


def ends_kernel(
    rank, g_ref, act_ref, dw_ref, vecs_ref, rate,
    delta_hbm, inside_hbm, before_hbm, pay_hbm,
    delta, inside_ref, before_ref, pay_ref, drive, b_all, cum_ref, ends, sems,
):
    rows, width = act_ref.shape
    steps = rows // CHUNKS
    halves = width // LANES
    z = jnp.dot(g_ref[:, :rank], dw_ref[...], preferred_element_type=F32) + vecs_ref[0:1, :]
    step_size = jnp.maximum(z, 0.0) + jnp.log1p(jnp.exp(-jnp.abs(z)))
    delta[...] = step_size
    pairs = ((delta, delta_hbm), (inside_ref, inside_hbm), (before_ref, before_hbm), (pay_ref, pay_hbm))
    copies = [pltpu.make_async_copy(source, target, sems.at[i]) for i, (source, target) in enumerate(pairs)]
    copies[0].start()
    drive[...] = step_size * act_ref[...]
    b_all[...] = jnp.dot(g_ref[:, rank:], spread(0, 2 * STATE), preferred_element_type=F32)
    chunk = lax.broadcasted_iota(jnp.int32, (CHUNKS, LANES), 0)
    zero = jnp.zeros((CHUNKS, LANES), F32)

    def add(step, totals):
        at = step_rows(step)
        totals = [totals[half] + delta[at, half * LANES : (half + 1) * LANES] for half in range(halves)]
        for half in range(halves):
            cum_ref[at, half * LANES : (half + 1) * LANES] = totals[half]
        return totals

    totals = lax.fori_loop(0, steps, add, [zero] * halves, unroll=8)
    for half in range(halves):
        cols = slice(half * LANES, (half + 1) * LANES)
        rates = [jnp.broadcast_to(rate[n : n + 1, cols], (CHUNKS, LANES)) for n in range(STATE)]
        total = totals[half]

        def gather(step, states, cols=cols, rates=rates, total=total):
            at = step_rows(step)
            left = total - cum_ref[at, cols]
            push = drive[at, cols]
            return [
                states[n] + jnp.exp2(left * rates[n]) * (push * b_all[at, n * LANES : (n + 1) * LANES])
                for n in range(STATE)
            ]

        states = lax.fori_loop(0, steps, gather, [zero] * STATE, unroll=8)
        sums = [total]
        shift = 1
        while shift < CHUNKS:
            sums.append(sums[-1] + jnp.where(chunk >= shift, pltpu.roll(sums[-1], shift, 0), 0.0))
            shift *= 2
        for n in range(STATE):
            end = states[n]
            shift = 1
            for level in range(len(sums) - 1):
                end = end + jnp.exp2(rates[n] * sums[level]) * jnp.where(
                    chunk >= shift, pltpu.roll(end, shift, 0), 0.0
                )
                shift *= 2
            inside_ref[n, :, cols] = jnp.where(chunk >= 1, pltpu.roll(end, 1, 0), 0.0)
            ends[n : n + 1, cols] = end[CHUNKS - 1 :, :]
        before_ref[:, cols] = jnp.where(chunk >= 1, pltpu.roll(sums[-1], 1, 0), 0.0)
        ends[STATE : STATE + 1, cols] = sums[-1][CHUNKS - 1 :, :]

    copies[1].start()
    copies[2].start()
    me = lax.axis_index("ctx")
    value = ends[0:STATE, :]
    total = jnp.broadcast_to(ends[STATE : STATE + 1, :], value.shape)
    high = total.astype(BF16).astype(F32)
    first = lax.broadcasted_iota(jnp.int32, value.shape, 0) == 0
    tail = jnp.where(first, high, total - high)
    for target in range(pay_ref.shape[0]):
        use = target > me
        pay_ref[target, 0:16, :] = jnp.where(use, value, 0.0).astype(BF16)
        pay_ref[target, 16:32, :] = jnp.where(use, tail, 0.0).astype(BF16)
    copies[3].start()
    for copy in copies:
        copy.wait()


def local_kernel(
    rank, g_ref, act_ref, rate, vecs_ref, delta_hbm, inside_hbm, before_hbm, gate_hbm,
    y_ref, cum_ref, lit_ref, spread_ref, maps_ref,
    b_all, c_all, delta, inside_ref, before_ref, gate_ref, sems,
):
    rows, width = act_ref.shape
    steps = rows // CHUNKS
    halves = width // LANES
    pairs = ((delta_hbm, delta), (inside_hbm, inside_ref), (before_hbm, before_ref), (gate_hbm, gate_ref))
    copies = [pltpu.make_async_copy(source, target, sems.at[i]) for i, (source, target) in enumerate(pairs)]
    for copy in copies:
        copy.start()
    b_all[...] = jnp.dot(g_ref[:, rank:], spread(0, 2 * STATE), preferred_element_type=F32)
    spread_ref[...] = spread(STATE, 2 * STATE)
    maps_ref[...] = g_ref[:, rank:]
    c_all[...] = jnp.dot(maps_ref[...], spread_ref[...], preferred_element_type=F32)
    for copy in copies:
        copy.wait()
    for half in range(halves):
        cols = slice(half * LANES, (half + 1) * LANES)
        rates = [jnp.broadcast_to(rate[n : n + 1, cols], (CHUNKS, LANES)) for n in range(STATE)]
        gain = vecs_ref[1:2, cols]

        def advance(step, carried, cols=cols, rates=rates, gain=gain):
            states, total = carried
            at = step_rows(step)
            size = delta[at, cols]
            value = act_ref[at, cols]
            push = size * value
            total = total + size
            out = gain * value
            later = []
            for n in range(STATE):
                group = slice(n * LANES, (n + 1) * LANES)
                now = jnp.exp2(size * rates[n]) * states[n] + push * b_all[at, group]
                out = out + c_all[at, group] * now
                later.append(now)
            y_ref[at, cols] = out
            cum_ref[at, cols] = total
            return later, total

        lax.fori_loop(
            0, steps, advance, ([inside_ref[n, :, cols] for n in range(STATE)], before_ref[:, cols]), unroll=4
        )
    lit_ref[...] = silu(gate_ref[...].astype(F32))


def finish_kernel(got_ref, maps_ref, spread_ref, y_ref, cum_ref, rate, lit_ref, out_hbm, c_all, carry, ys, out_ref, sems):
    rows, width = y_ref.shape
    steps = rows // CHUNKS
    halves = width // LANES
    c_all[...] = jnp.dot(maps_ref[...], spread_ref[...], preferred_element_type=F32)
    incoming = jnp.zeros((STATE, width), F32)
    for source in range(got_ref.shape[0] - 1):
        tail = got_ref[source, 16:32, :].astype(F32)
        decay = jnp.exp2(rate[...] * (tail[0:1, :] + tail[1:2, :]))
        incoming = decay * incoming + got_ref[source, 0:16, :].astype(F32)
    carry[...] = incoming
    leaving = []
    for half in range(halves):
        cols = slice(half * LANES, (half + 1) * LANES)
        rates = [jnp.broadcast_to(rate[n : n + 1, cols], (CHUNKS, LANES)) for n in range(STATE)]
        entering = [jnp.broadcast_to(carry[n : n + 1, cols], (CHUNKS, LANES)) for n in range(STATE)]

        def correct(step, _, half=half, cols=cols, rates=rates, entering=entering):
            at = step_rows(step)
            total = cum_ref[at, cols]
            out = y_ref[at, cols]
            for n in range(STATE):
                group = slice(n * LANES, (n + 1) * LANES)
                out = out + (c_all[at, group] * entering[n]) * jnp.exp2(total * rates[n])
            ys[half, pl.ds(step, CHUNKS, stride=steps), :] = out
            return 0

        lax.fori_loop(0, steps, correct, 0, unroll=8)
        out_ref[half] = (ys[half] * lit_ref[:, cols]).astype(BF16)
        copy = pltpu.make_async_copy(out_ref.at[half], out_hbm.at[:, cols], sems.at[half])
        copy.start()
        leaving.append(copy)
    for copy in leaving:
        copy.wait()


def on_device(
    mamba_in, mamba_gate, conv_weight, conv_bias, proj_delta, proj_select, delta_weight, delta_bias, decay_log, skip_gain,
):
    rows, width = mamba_in.shape
    rank = proj_delta.shape[1]
    maps = proj_select.shape[1]
    halves = width // LANES
    steps = rows // CHUNKS
    n_ctx, n_ch = lax.axis_size("ctx"), lax.axis_size("ch")
    wide = rank + LANES
    cells = rows * width * STATE
    tile = jax.ShapeDtypeStruct((rows, width), F32)
    part_shape = jax.ShapeDtypeStruct((rows, wide), BF16)
    big = pltpu.VMEM((rows, STATE * LANES), F32)

    halo = lax.ppermute(mamba_in[rows - 16 :], "ctx", [(i, i + 1) for i in range(n_ctx - 1)])
    act, part, head, pd, sel, taps, dw, rate, vecs = pl.pallas_call(
        project_kernel,
        out_shape=(
            tile,
            part_shape,
            jax.ShapeDtypeStruct((8, width), F32),
            jax.ShapeDtypeStruct(proj_delta.shape, BF16),
            jax.ShapeDtypeStruct((LANES, width), BF16),
            jax.ShapeDtypeStruct((8, width), F32),
            jax.ShapeDtypeStruct(delta_weight.shape, BF16),
            jax.ShapeDtypeStruct((STATE, width), F32),
            jax.ShapeDtypeStruct((8, width), F32),
        ),
        in_specs=hbm(9),
        out_specs=tuple(vmem(9)),
        scratch_shapes=[
            pltpu.VMEM((rows, width), BF16),
            pltpu.VMEM((STATE, width), F32),
            pltpu.VMEM((KWIDTH, width), F32),
            pltpu.VMEM((1, width), F32),
            pltpu.VMEM((maps, width), BF16),
            pltpu.VMEM((halves, rows + 8, LANES), F32),
            pltpu.VMEM((halves, (steps + KWIDTH - 1) * CHUNKS, LANES), F32),
            pltpu.VMEM((rows, width), BF16),
            pltpu.SemaphoreType.DMA((9,)),
        ],
        compiler_params=pltpu.CompilerParams(vmem_limit_bytes=16 * MIB),
        cost_estimate=pl.CostEstimate(
            flops=2 * rows * width * wide, bytes_accessed=2 * rows * width * 8, transcendentals=rows * width
        ),
        name="project",
    )(
        *stay(
            mamba_in, proj_delta, proj_select.T, conv_weight, conv_bias[None, :],
            delta_weight, decay_log, delta_bias[None, :], skip_gain[None, :],
        )
    )
    act, part = pl.pallas_call(
        functools.partial(head_kernel, maps),
        out_shape=(tile, part_shape),
        in_specs=vmem(7),
        out_specs=tuple(vmem(2)),
        scratch_shapes=[pltpu.VMEM((16, width), F32)],
        compiler_params=pltpu.CompilerParams(vmem_limit_bytes=16 * MIB),
        name="first_rows",
    )(halo, head, taps, pd, sel, act, part)

    parts = lax.all_to_all(part.reshape(n_ch, rows // n_ch, wide), "ch", 0, 0)
    totals = pl.pallas_call(
        functools.partial(total_kernel, rank, maps),
        out_shape=jax.ShapeDtypeStruct(parts.shape, BF16),
        in_specs=vmem(1),
        out_specs=vmem(1)[0],
        compiler_params=pltpu.CompilerParams(vmem_limit_bytes=16 * MIB),
        name="total",
    )(parts)
    gathered = lax.all_to_all(totals, "ch", 0, 0).reshape(rows, wide)

    sent = (
        ((rows, width), F32),
        ((STATE, CHUNKS, width), F32),
        ((CHUNKS, width), F32),
        ((n_ctx, 2 * STATE, width), BF16),
    )
    delta, inside, before, pay = pl.pallas_call(
        functools.partial(ends_kernel, rank),
        out_shape=tuple(pltpu.HBM(*kept) for kept in sent),
        in_specs=vmem(5),
        out_specs=tuple(hbm(4)),
        scratch_shapes=[
            *(pltpu.VMEM(*kept) for kept in sent),
            pltpu.VMEM((rows, width), F32),
            big,
            pltpu.VMEM((rows, width), F32),
            pltpu.VMEM((STATE + 8, width), F32),
            pltpu.SemaphoreType.DMA((4,)),
        ],
        compiler_params=pltpu.CompilerParams(vmem_limit_bytes=16 * MIB),
        name="ends",
    )(gathered, act, dw, vecs, rate)

    got = lax.all_to_all(pay, "ctx", 0, 0)
    y_local, cum, lit, spread_c, maps_all = pl.pallas_call(
        functools.partial(local_kernel, rank),
        out_shape=(
            tile,
            tile,
            tile,
            jax.ShapeDtypeStruct((LANES, STATE * LANES), BF16),
            jax.ShapeDtypeStruct((rows, LANES), BF16),
        ),
        in_specs=vmem(4) + hbm(4),
        out_specs=tuple(vmem(5)),
        scratch_shapes=[
            big,
            big,
            *(pltpu.VMEM(*kept) for kept in sent[:3]),
            pltpu.VMEM((rows, width), BF16),
            pltpu.SemaphoreType.DMA((4,)),
        ],
        compiler_params=pltpu.CompilerParams(vmem_limit_bytes=24 * MIB),
        cost_estimate=pl.CostEstimate(flops=6 * cells, bytes_accessed=8 * rows * width * 4, transcendentals=cells),
        name="local_scan",
    )(gathered, act, rate, vecs, *stay(delta, inside, before, mamba_gate))
    return pl.pallas_call(
        finish_kernel,
        out_shape=jax.ShapeDtypeStruct((rows, width), BF16),
        in_specs=vmem(7),
        out_specs=hbm(1)[0],
        scratch_shapes=[
            big,
            pltpu.VMEM((STATE, width), F32),
            pltpu.VMEM((halves, rows, LANES), F32),
            pltpu.VMEM((halves, rows, LANES), BF16),
            pltpu.SemaphoreType.DMA((halves,)),
        ],
        compiler_params=pltpu.CompilerParams(vmem_limit_bytes=16 * MIB),
        name="finish",
    )(got, maps_all, spread_c, y_local, cum, rate, lit)


def solution(mesh):
    return jax.shard_map(
        on_device,
        mesh=mesh,
        in_specs=(
            P("ctx", "ch"),
            P("ctx", "ch"),
            P(None, "ch"),
            P("ch"),
            P("ch", None),
            P("ch", None),
            P(None, "ch"),
            P("ch"),
            P(None, "ch"),
            P("ch"),
        ),
        out_specs=P("ctx", "ch"),
        check_vma=False,
    )
```

```python
import functools
import math

import jax
import jax.numpy as jnp
from jax import lax
from jax.experimental import pallas as pl
from jax.experimental.pallas import tpu as pltpu
from jax.sharding import PartitionSpec as P

STATE = 16
KWIDTH = 4
LANES = 128
CHUNKS = 8
HEAD = 32
LOG2E = 1.0 / math.log(2.0)
MIB = 1 << 20
F32 = jnp.float32
BF16 = jnp.bfloat16


def vmem(count):
    return [pl.BlockSpec(memory_space=pltpu.VMEM)] * count


def hbm(count):
    return [pl.BlockSpec(memory_space=pltpu.HBM)] * count


def stay(*arrays):
    return [pltpu.with_memory_space_constraint(array, pltpu.HBM) for array in arrays]


def silu(value):
    return value / (1.0 + jnp.exp(-value))


def put_products(low, pd, sel, maps, rank, part_ref, rows):
    part_ref[rows, 0:rank] = jnp.dot(low, pd, preferred_element_type=F32).astype(BF16)
    both = lax.dot_general(low, sel, (((1,), (1,)), ((), ())), preferred_element_type=F32)
    high = both.astype(BF16).astype(F32)
    lane = lax.broadcasted_iota(jnp.int32, both.shape, 1)
    part_ref[rows, rank : rank + LANES] = jnp.where(lane < maps, high, both - high).astype(BF16)


def project_kernel(
    x_hbm, pd_hbm, ps_hbm, weight_hbm, bias_hbm, dw_hbm, log_hbm, dbias_hbm, gain_hbm,
    act_ref, part_ref, head_ref, pd_ref, sel_ref, taps_ref, dw_ref, rate_ref, vecs_ref,
    x_ref, log_ref, weight_ref, bias_ref, ps_ref, xs, xp, low, sems,
):
    rows, width = x_ref.shape
    steps = rows // CHUNKS
    rank = pd_ref.shape[1]
    maps = ps_ref.shape[0]
    halves = width // LANES
    pairs = (
        (x_hbm, x_ref), (weight_hbm, weight_ref), (bias_hbm, bias_ref), (ps_hbm, ps_ref), (pd_hbm, pd_ref),
        (log_hbm, log_ref), (dw_hbm, dw_ref), (dbias_hbm, vecs_ref.at[0:1]), (gain_hbm, vecs_ref.at[1:2]),
    )
    copies = [pltpu.make_async_copy(source, target, sems.at[i]) for i, (source, target) in enumerate(pairs)]
    for copy in copies:
        copy.start()
    copies[0].wait()
    head_ref[...] = x_ref[0:16, :].astype(F32)[0:8, :]
    for half in range(halves):
        cols = slice(half * LANES, (half + 1) * LANES)
        xs[half, 0:8, :] = jnp.zeros((8, LANES), F32)
        xs[half, 8 : 8 + rows, :] = x_ref[:, cols].astype(F32)
        for step in range(-(KWIDTH - 1), steps):
            to = (step + KWIDTH - 1) * CHUNKS
            xp[half, to : to + CHUNKS, :] = xs[half, pl.ds(8 + step, CHUNKS, stride=steps), :]
    copies[1].wait()
    copies[2].wait()
    taps_ref[0:KWIDTH, :] = weight_ref[...]
    taps_ref[KWIDTH : KWIDTH + 1, :] = bias_ref[...]
    block = min(rows, 64)
    for half in range(halves):
        cols = slice(half * LANES, (half + 1) * LANES)
        for start in range(0, rows, block):
            value = bias_ref[:, cols]
            for tap in range(KWIDTH):
                at = start + tap * CHUNKS
                value = value + weight_ref[tap : tap + 1, cols] * xp[half, at : at + block, :]
            value = silu(value)
            act_ref[start : start + block, cols] = value
            low[start : start + block, cols] = value.astype(BF16)
    copies[3].wait()
    sel_ref[...] = jnp.zeros_like(sel_ref)
    sel_ref[0:maps, :] = ps_ref[...]
    sel_ref[maps : 2 * maps, :] = ps_ref[...]
    copies[4].wait()
    put_products(low[...], pd_ref[...], sel_ref[...], maps, rank, part_ref, slice(0, rows))
    copies[5].wait()
    rate_ref[...] = -jnp.exp(log_ref[...]) * LOG2E
    for copy in copies[6:]:
        copy.wait()


def head_kernel(maps, halo_ref, head_ref, taps_ref, pd_ref, sel_ref, act_in, part_in, act_ref, part_ref, ext):
    rank = pd_ref.shape[1]
    ext[0:8, :] = halo_ref[...].astype(F32)[-8:, :]
    ext[8:16, :] = head_ref[...]
    value = taps_ref[KWIDTH : KWIDTH + 1, :]
    for tap in range(KWIDTH):
        at = 8 - (KWIDTH - 1) + tap
        value = value + taps_ref[tap : tap + 1, :] * ext[at : at + 8, :]
    value = silu(value)
    act_ref[...] = act_in[...]
    part_ref[...] = part_in[...]
    for token in range(KWIDTH - 1):
        act_ref[token * CHUNKS : token * CHUNKS + 1, :] = value[token : token + 1, :]
    low = act_ref[0:HEAD, :].astype(BF16)
    put_products(low, pd_ref[...], sel_ref[...], maps, rank, part_ref, slice(0, HEAD))


def total_kernel(parts_ref, out_ref):
    total = parts_ref[0].astype(F32)
    for source in range(1, parts_ref.shape[0]):
        total = total + parts_ref[source].astype(F32)
    out_ref[...] = total


def share_kernel(rank, maps, mine_ref, other_ref, out_ref):
    total = mine_ref[...] + other_ref[...]
    chosen = total[:, rank:]
    lane = lax.broadcasted_iota(jnp.int32, chosen.shape, 1)
    summed = chosen + pltpu.roll(chosen, LANES - maps, 1)
    twice = jnp.where(lane < maps, summed, pltpu.roll(summed, maps, 1))
    high = twice.astype(BF16).astype(F32)
    rest = jnp.where(lane < 2 * maps, twice - high, 0.0)
    mixed = jnp.where(lane < maps, high, rest)
    row = jnp.concatenate([total[:, :rank], mixed], axis=1).astype(BF16)
    for target in range(out_ref.shape[0]):
        out_ref[target] = row


def spread(first, maps):
    shape = (LANES, STATE * LANES)
    source = lax.broadcasted_iota(jnp.int32, shape, 0)
    group = lax.broadcasted_iota(jnp.int32, shape, 1) >> 7
    hit = (source == group + first) | (source == group + (first + maps))
    return jnp.where(hit, 1.0, 0.0).astype(BF16)


def step_rows(step):
    return pl.ds(pl.multiple_of(step * CHUNKS, CHUNKS), CHUNKS)


def ends_kernel(
    rank, g_ref, act_ref, dw_ref, vecs_ref, rate,
    delta_hbm, inside_hbm, before_hbm, pay_hbm,
    delta, inside_ref, before_ref, pay_ref, drive, b_all, cum_ref, ends, sems,
):
    rows, width = act_ref.shape
    steps = rows // CHUNKS
    halves = width // LANES
    z = jnp.dot(g_ref[:, :rank], dw_ref[...], preferred_element_type=F32) + vecs_ref[0:1, :]
    step_size = jnp.maximum(z, 0.0) + jnp.log1p(jnp.exp(-jnp.abs(z)))
    delta[...] = step_size
    pairs = ((delta, delta_hbm), (inside_ref, inside_hbm), (before_ref, before_hbm), (pay_ref, pay_hbm))
    copies = [pltpu.make_async_copy(source, target, sems.at[i]) for i, (source, target) in enumerate(pairs)]
    copies[0].start()
    drive[...] = step_size * act_ref[...]
    b_all[...] = jnp.dot(g_ref[:, rank:], spread(0, 2 * STATE), preferred_element_type=F32)
    chunk = lax.broadcasted_iota(jnp.int32, (CHUNKS, LANES), 0)
    zero = jnp.zeros((CHUNKS, LANES), F32)

    def add(step, totals):
        at = step_rows(step)
        totals = [totals[half] + delta[at, half * LANES : (half + 1) * LANES] for half in range(halves)]
        for half in range(halves):
            cum_ref[at, half * LANES : (half + 1) * LANES] = totals[half]
        return totals

    totals = lax.fori_loop(0, steps, add, [zero] * halves, unroll=8)
    for half in range(halves):
        cols = slice(half * LANES, (half + 1) * LANES)
        rates = [jnp.broadcast_to(rate[n : n + 1, cols], (CHUNKS, LANES)) for n in range(STATE)]
        total = totals[half]

        def gather(step, states, cols=cols, rates=rates, total=total):
            at = step_rows(step)
            left = total - cum_ref[at, cols]
            push = drive[at, cols]
            return [
                states[n] + jnp.exp2(left * rates[n]) * (push * b_all[at, n * LANES : (n + 1) * LANES])
                for n in range(STATE)
            ]

        states = lax.fori_loop(0, steps, gather, [zero] * STATE, unroll=8)
        sums = [total]
        shift = 1
        while shift < CHUNKS:
            sums.append(sums[-1] + jnp.where(chunk >= shift, pltpu.roll(sums[-1], shift, 0), 0.0))
            shift *= 2
        for n in range(STATE):
            end = states[n]
            shift = 1
            for level in range(len(sums) - 1):
                end = end + jnp.exp2(rates[n] * sums[level]) * jnp.where(
                    chunk >= shift, pltpu.roll(end, shift, 0), 0.0
                )
                shift *= 2
            inside_ref[n, :, cols] = jnp.where(chunk >= 1, pltpu.roll(end, 1, 0), 0.0)
            ends[n : n + 1, cols] = end[CHUNKS - 1 :, :]
        before_ref[:, cols] = jnp.where(chunk >= 1, pltpu.roll(sums[-1], 1, 0), 0.0)
        ends[STATE : STATE + 1, cols] = sums[-1][CHUNKS - 1 :, :]

    copies[1].start()
    copies[2].start()
    me = lax.axis_index("ctx")
    value = ends[0:STATE, :]
    total = jnp.broadcast_to(ends[STATE : STATE + 1, :], value.shape)
    high = total.astype(BF16).astype(F32)
    first = lax.broadcasted_iota(jnp.int32, value.shape, 0) == 0
    tail = jnp.where(first, high, total - high)
    for target in range(pay_ref.shape[0]):
        use = target > me
        pay_ref[target, 0:16, :] = jnp.where(use, value, 0.0).astype(BF16)
        pay_ref[target, 16:32, :] = jnp.where(use, tail, 0.0).astype(BF16)
    copies[3].start()
    for copy in copies:
        copy.wait()


def local_kernel(
    rank, g_ref, act_ref, rate, vecs_ref, delta_hbm, inside_hbm, before_hbm, gate_hbm,
    y_ref, cum_ref, lit_ref, spread_ref, maps_ref,
    b_all, c_all, delta, inside_ref, before_ref, gate_ref, sems,
):
    rows, width = act_ref.shape
    steps = rows // CHUNKS
    halves = width // LANES
    pairs = ((delta_hbm, delta), (inside_hbm, inside_ref), (before_hbm, before_ref), (gate_hbm, gate_ref))
    copies = [pltpu.make_async_copy(source, target, sems.at[i]) for i, (source, target) in enumerate(pairs)]
    for copy in copies:
        copy.start()
    b_all[...] = jnp.dot(g_ref[:, rank:], spread(0, 2 * STATE), preferred_element_type=F32)
    spread_ref[...] = spread(STATE, 2 * STATE)
    maps_ref[...] = g_ref[:, rank:]
    c_all[...] = jnp.dot(maps_ref[...], spread_ref[...], preferred_element_type=F32)
    for copy in copies:
        copy.wait()
    for half in range(halves):
        cols = slice(half * LANES, (half + 1) * LANES)
        rates = [jnp.broadcast_to(rate[n : n + 1, cols], (CHUNKS, LANES)) for n in range(STATE)]
        gain = vecs_ref[1:2, cols]

        def advance(step, carried, cols=cols, rates=rates, gain=gain):
            states, total = carried
            at = step_rows(step)
            size = delta[at, cols]
            value = act_ref[at, cols]
            push = size * value
            total = total + size
            out = gain * value
            later = []
            for n in range(STATE):
                group = slice(n * LANES, (n + 1) * LANES)
                now = jnp.exp2(size * rates[n]) * states[n] + push * b_all[at, group]
                out = out + c_all[at, group] * now
                later.append(now)
            y_ref[at, cols] = out
            cum_ref[at, cols] = total
            return later, total

        lax.fori_loop(
            0, steps, advance, ([inside_ref[n, :, cols] for n in range(STATE)], before_ref[:, cols]), unroll=4
        )
    lit_ref[...] = silu(gate_ref[...].astype(F32))


def finish_kernel(got_ref, maps_ref, spread_ref, y_ref, cum_ref, rate, lit_ref, out_hbm, c_all, carry, ys, out_ref, sems):
    rows, width = y_ref.shape
    steps = rows // CHUNKS
    halves = width // LANES
    c_all[...] = jnp.dot(maps_ref[...], spread_ref[...], preferred_element_type=F32)
    incoming = jnp.zeros((STATE, width), F32)
    for source in range(got_ref.shape[0] - 1):
        tail = got_ref[source, 16:32, :].astype(F32)
        decay = jnp.exp2(rate[...] * (tail[0:1, :] + tail[1:2, :]))
        incoming = decay * incoming + got_ref[source, 0:16, :].astype(F32)
    carry[...] = incoming
    leaving = []
    for half in range(halves):
        cols = slice(half * LANES, (half + 1) * LANES)
        rates = [jnp.broadcast_to(rate[n : n + 1, cols], (CHUNKS, LANES)) for n in range(STATE)]
        entering = [jnp.broadcast_to(carry[n : n + 1, cols], (CHUNKS, LANES)) for n in range(STATE)]

        def correct(step, _, half=half, cols=cols, rates=rates, entering=entering):
            at = step_rows(step)
            total = cum_ref[at, cols]
            out = y_ref[at, cols]
            for n in range(STATE):
                group = slice(n * LANES, (n + 1) * LANES)
                out = out + (c_all[at, group] * entering[n]) * jnp.exp2(total * rates[n])
            ys[half, pl.ds(step, CHUNKS, stride=steps), :] = out
            return 0

        lax.fori_loop(0, steps, correct, 0, unroll=8)
        out_ref[half] = (ys[half] * lit_ref[:, cols]).astype(BF16)
        copy = pltpu.make_async_copy(out_ref.at[half], out_hbm.at[:, cols], sems.at[half])
        copy.start()
        leaving.append(copy)
    for copy in leaving:
        copy.wait()


def on_device(
    mamba_in, mamba_gate, conv_weight, conv_bias, proj_delta, proj_select, delta_weight, delta_bias, decay_log, skip_gain,
):
    rows, width = mamba_in.shape
    rank = proj_delta.shape[1]
    maps = proj_select.shape[1]
    halves = width // LANES
    steps = rows // CHUNKS
    n_ctx, n_ch = lax.axis_size("ctx"), lax.axis_size("ch")
    wide = rank + LANES
    cells = rows * width * STATE
    tile = jax.ShapeDtypeStruct((rows, width), F32)
    part_shape = jax.ShapeDtypeStruct((rows, wide), BF16)
    big = pltpu.VMEM((rows, STATE * LANES), F32)

    halo = lax.ppermute(mamba_in[rows - 16 :], "ctx", [(i, i + 1) for i in range(n_ctx - 1)])
    act, part, head, pd, sel, taps, dw, rate, vecs = pl.pallas_call(
        project_kernel,
        out_shape=(
            tile,
            part_shape,
            jax.ShapeDtypeStruct((8, width), F32),
            jax.ShapeDtypeStruct(proj_delta.shape, BF16),
            jax.ShapeDtypeStruct((LANES, width), BF16),
            jax.ShapeDtypeStruct((8, width), F32),
            jax.ShapeDtypeStruct(delta_weight.shape, BF16),
            jax.ShapeDtypeStruct((STATE, width), F32),
            jax.ShapeDtypeStruct((8, width), F32),
        ),
        in_specs=hbm(9),
        out_specs=tuple(vmem(9)),
        scratch_shapes=[
            pltpu.VMEM((rows, width), BF16),
            pltpu.VMEM((STATE, width), F32),
            pltpu.VMEM((KWIDTH, width), F32),
            pltpu.VMEM((1, width), F32),
            pltpu.VMEM((maps, width), BF16),
            pltpu.VMEM((halves, rows + 8, LANES), F32),
            pltpu.VMEM((halves, (steps + KWIDTH - 1) * CHUNKS, LANES), F32),
            pltpu.VMEM((rows, width), BF16),
            pltpu.SemaphoreType.DMA((9,)),
        ],
        compiler_params=pltpu.CompilerParams(vmem_limit_bytes=16 * MIB),
        cost_estimate=pl.CostEstimate(
            flops=2 * rows * width * wide, bytes_accessed=2 * rows * width * 8, transcendentals=rows * width
        ),
        name="project",
    )(
        *stay(
            mamba_in, proj_delta, proj_select.T, conv_weight, conv_bias[None, :],
            delta_weight, decay_log, delta_bias[None, :], skip_gain[None, :],
        )
    )
    act, part = pl.pallas_call(
        functools.partial(head_kernel, maps),
        out_shape=(tile, part_shape),
        in_specs=vmem(7),
        out_specs=tuple(vmem(2)),
        scratch_shapes=[pltpu.VMEM((16, width), F32)],
        compiler_params=pltpu.CompilerParams(vmem_limit_bytes=16 * MIB),
        name="first_rows",
    )(halo, head, taps, pd, sel, act, part)

    near = n_ch // 2
    groups = [list(range(near)), list(range(near, n_ch))]
    own = rows // near
    parts = lax.all_to_all(part.reshape(near, own, wide), "ch", 0, 0, axis_index_groups=groups)
    mine = pl.pallas_call(
        total_kernel,
        out_shape=jax.ShapeDtypeStruct((own, wide), F32),
        in_specs=vmem(1),
        out_specs=vmem(1)[0],
        compiler_params=pltpu.CompilerParams(vmem_limit_bytes=16 * MIB),
        name="total",
    )(parts)
    other = lax.ppermute(mine, "ch", [(i, (i + near) % n_ch) for i in range(n_ch)])
    totals = pl.pallas_call(
        functools.partial(share_kernel, rank, maps),
        out_shape=jax.ShapeDtypeStruct(parts.shape, BF16),
        in_specs=vmem(2),
        out_specs=vmem(1)[0],
        compiler_params=pltpu.CompilerParams(vmem_limit_bytes=16 * MIB),
        name="share",
    )(mine, other)
    gathered = lax.all_to_all(totals, "ch", 0, 0, axis_index_groups=groups).reshape(rows, wide)

    sent = (
        ((rows, width), F32),
        ((STATE, CHUNKS, width), F32),
        ((CHUNKS, width), F32),
        ((n_ctx, 2 * STATE, width), BF16),
    )
    delta, inside, before, pay = pl.pallas_call(
        functools.partial(ends_kernel, rank),
        out_shape=tuple(pltpu.HBM(*kept) for kept in sent),
        in_specs=vmem(5),
        out_specs=tuple(hbm(4)),
        scratch_shapes=[
            *(pltpu.VMEM(*kept) for kept in sent),
            pltpu.VMEM((rows, width), F32),
            big,
            pltpu.VMEM((rows, width), F32),
            pltpu.VMEM((STATE + 8, width), F32),
            pltpu.SemaphoreType.DMA((4,)),
        ],
        compiler_params=pltpu.CompilerParams(vmem_limit_bytes=16 * MIB),
        name="ends",
    )(gathered, act, dw, vecs, rate)

    got = lax.all_to_all(pay, "ctx", 0, 0)
    y_local, cum, lit, spread_c, maps_all = pl.pallas_call(
        functools.partial(local_kernel, rank),
        out_shape=(
            tile,
            tile,
            tile,
            jax.ShapeDtypeStruct((LANES, STATE * LANES), BF16),
            jax.ShapeDtypeStruct((rows, LANES), BF16),
        ),
        in_specs=vmem(4) + hbm(4),
        out_specs=tuple(vmem(5)),
        scratch_shapes=[
            big,
            big,
            *(pltpu.VMEM(*kept) for kept in sent[:3]),
            pltpu.VMEM((rows, width), BF16),
            pltpu.SemaphoreType.DMA((4,)),
        ],
        compiler_params=pltpu.CompilerParams(vmem_limit_bytes=24 * MIB),
        cost_estimate=pl.CostEstimate(flops=6 * cells, bytes_accessed=8 * rows * width * 4, transcendentals=cells),
        name="local_scan",
    )(gathered, act, rate, vecs, *stay(delta, inside, before, mamba_gate))
    return pl.pallas_call(
        finish_kernel,
        out_shape=jax.ShapeDtypeStruct((rows, width), BF16),
        in_specs=vmem(7),
        out_specs=hbm(1)[0],
        scratch_shapes=[
            big,
            pltpu.VMEM((STATE, width), F32),
            pltpu.VMEM((halves, rows, LANES), F32),
            pltpu.VMEM((halves, rows, LANES), BF16),
            pltpu.SemaphoreType.DMA((halves,)),
        ],
        compiler_params=pltpu.CompilerParams(vmem_limit_bytes=16 * MIB),
        name="finish",
    )(got, maps_all, spread_c, y_local, cum, rate, lit)


def solution(mesh):
    return jax.shard_map(
        on_device,
        mesh=mesh,
        in_specs=(
            P("ctx", "ch"),
            P("ctx", "ch"),
            P(None, "ch"),
            P("ch"),
            P("ch", None),
            P("ch", None),
            P(None, "ch"),
            P("ch"),
            P(None, "ch"),
            P("ch"),
        ),
        out_specs=P("ctx", "ch"),
        check_vma=False,
    )
```

```python
import functools
import math

import jax
import jax.numpy as jnp
from jax import lax
from jax.experimental import pallas as pl
from jax.experimental.pallas import tpu as pltpu
from jax.sharding import PartitionSpec as P

STATE = 16
KWIDTH = 4
LANES = 128
CHUNKS = 8
HEAD = 32
LOG2E = 1.0 / math.log(2.0)
MIB = 1 << 20
F32 = jnp.float32
BF16 = jnp.bfloat16


def vmem(count):
    return [pl.BlockSpec(memory_space=pltpu.VMEM)] * count


def hbm(count):
    return [pl.BlockSpec(memory_space=pltpu.HBM)] * count


def stay(*arrays):
    return [pltpu.with_memory_space_constraint(array, pltpu.HBM) for array in arrays]


def silu(value):
    return value / (1.0 + jnp.exp(-value))


def put_products(low, pd, sel, maps, rank, part_ref, rows):
    part_ref[rows, 0:rank] = jnp.dot(low, pd, preferred_element_type=F32).astype(BF16)
    both = lax.dot_general(low, sel, (((1,), (1,)), ((), ())), preferred_element_type=F32)
    high = both.astype(BF16).astype(F32)
    lane = lax.broadcasted_iota(jnp.int32, both.shape, 1)
    part_ref[rows, rank : rank + LANES] = jnp.where(lane < maps, high, both - high).astype(BF16)


def project_kernel(
    x_hbm, pd_hbm, ps_hbm, weight_hbm, bias_hbm, dw_hbm, log_hbm, dbias_hbm,
    act_ref, part_ref, head_ref, pd_ref, sel_ref, taps_ref, dw_ref, rate_ref, vecs_ref,
    x_ref, log_ref, weight_ref, bias_ref, ps_ref, xs, xp, low, sems,
):
    rows, width = x_ref.shape
    steps = rows // CHUNKS
    rank = pd_ref.shape[1]
    maps = ps_ref.shape[0]
    halves = width // LANES
    pairs = (
        (x_hbm, x_ref), (weight_hbm, weight_ref), (bias_hbm, bias_ref), (ps_hbm, ps_ref), (pd_hbm, pd_ref),
        (log_hbm, log_ref), (dw_hbm, dw_ref), (dbias_hbm, vecs_ref.at[0:1]),
    )
    copies = [pltpu.make_async_copy(source, target, sems.at[i]) for i, (source, target) in enumerate(pairs)]
    for copy in copies:
        copy.start()
    copies[0].wait()
    head_ref[...] = x_ref[0:16, :].astype(F32)[0:8, :]
    for half in range(halves):
        cols = slice(half * LANES, (half + 1) * LANES)
        xs[half, 0:8, :] = jnp.zeros((8, LANES), F32)
        xs[half, 8 : 8 + rows, :] = x_ref[:, cols].astype(F32)
        for step in range(-(KWIDTH - 1), steps):
            to = (step + KWIDTH - 1) * CHUNKS
            xp[half, to : to + CHUNKS, :] = xs[half, pl.ds(8 + step, CHUNKS, stride=steps), :]
    copies[1].wait()
    copies[2].wait()
    taps_ref[0:KWIDTH, :] = weight_ref[...]
    taps_ref[KWIDTH : KWIDTH + 1, :] = bias_ref[...]
    block = min(rows, 64)
    for half in range(halves):
        cols = slice(half * LANES, (half + 1) * LANES)
        for start in range(0, rows, block):
            value = bias_ref[:, cols]
            for tap in range(KWIDTH):
                at = start + tap * CHUNKS
                value = value + weight_ref[tap : tap + 1, cols] * xp[half, at : at + block, :]
            value = silu(value)
            act_ref[start : start + block, cols] = value
            low[start : start + block, cols] = value.astype(BF16)
    copies[3].wait()
    sel_ref[...] = jnp.zeros_like(sel_ref)
    sel_ref[0:maps, :] = ps_ref[...]
    sel_ref[maps : 2 * maps, :] = ps_ref[...]
    copies[4].wait()
    put_products(low[...], pd_ref[...], sel_ref[...], maps, rank, part_ref, slice(0, rows))
    copies[5].wait()
    rate_ref[...] = -jnp.exp(log_ref[...]) * LOG2E
    for copy in copies[6:]:
        copy.wait()


def head_kernel(maps, halo_ref, head_ref, taps_ref, pd_ref, sel_ref, act_in, part_in, act_ref, part_ref, ext):
    rank = pd_ref.shape[1]
    ext[0:8, :] = halo_ref[...].astype(F32)[-8:, :]
    ext[8:16, :] = head_ref[...]
    value = taps_ref[KWIDTH : KWIDTH + 1, :]
    for tap in range(KWIDTH):
        at = 8 - (KWIDTH - 1) + tap
        value = value + taps_ref[tap : tap + 1, :] * ext[at : at + 8, :]
    value = silu(value)
    act_ref[...] = act_in[...]
    part_ref[...] = part_in[...]
    for token in range(KWIDTH - 1):
        act_ref[token * CHUNKS : token * CHUNKS + 1, :] = value[token : token + 1, :]
    low = act_ref[0:HEAD, :].astype(BF16)
    put_products(low, pd_ref[...], sel_ref[...], maps, rank, part_ref, slice(0, HEAD))


def fold(chosen, maps):
    lane = lax.broadcasted_iota(jnp.int32, chosen.shape, 1)
    summed = chosen + pltpu.roll(chosen, LANES - maps, 1)
    twice = jnp.where(lane < maps, summed, pltpu.roll(summed, maps, 1))
    return jnp.where(lane < 2 * maps, twice, 0.0)


def parted(twice, maps):
    lane = lax.broadcasted_iota(jnp.int32, twice.shape, 1)
    high = twice.astype(BF16).astype(F32)
    return jnp.where(lane < maps, high, twice - high).astype(BF16)


def total_kernel(rank, maps, parts_ref, mine_ref, send_ref):
    total = parts_ref[0].astype(F32)
    for source in range(1, parts_ref.shape[0]):
        total = total + parts_ref[source].astype(F32)
    twice = fold(total[:, rank:], maps)
    mine_ref[:, :rank] = total[:, :rank]
    mine_ref[:, rank:] = twice
    send_ref[:, :rank] = total[:, :rank].astype(BF16)
    send_ref[:, rank:] = parted(twice, maps)


def share_kernel(rank, maps, mine_ref, other_ref, ready_ref, out_ref):
    other = other_ref[...].astype(F32)
    low = (mine_ref[:, :rank] + other[:, :rank]).astype(BF16)
    chosen = parted(mine_ref[:, rank:] + fold(other[:, rank:], maps), maps)
    for target in range(out_ref.shape[0]):
        out_ref[target, :, :rank] = low
        out_ref[target, :, rank:] = chosen


def ready_kernel(mine_ref, gate_hbm, lit_ref, spread_ref, done_ref, gate_ref, sem):
    copy = pltpu.make_async_copy(gate_hbm, gate_ref, sem)
    copy.start()
    source = lax.broadcasted_iota(jnp.int32, spread_ref.shape, 0)
    group = lax.broadcasted_iota(jnp.int32, spread_ref.shape, 1) >> 7
    hit = (source == group) | (source == group + 2 * STATE)
    spread_ref[...] = jnp.where(hit, 1.0, 0.0).astype(BF16)
    done_ref[...] = jnp.zeros_like(done_ref)
    copy.wait()
    lit_ref[...] = silu(gate_ref[...].astype(F32))


def step_rows(step):
    return pl.ds(pl.multiple_of(step * CHUNKS, CHUNKS), CHUNKS)


def ends_kernel(
    rank, g_ref, act_ref, dw_ref, vecs_ref, rate, spread_ref,
    delta_hbm, inside_hbm, before_hbm, pay_hbm,
    delta, inside_ref, before_ref, pay_ref, drive, b_all, cum_ref, ends, sems,
):
    rows, width = act_ref.shape
    steps = rows // CHUNKS
    halves = width // LANES
    z = jnp.dot(g_ref[:, :rank], dw_ref[...], preferred_element_type=F32) + vecs_ref[0:1, :]
    step_size = jnp.maximum(z, 0.0) + jnp.log1p(jnp.exp(-jnp.abs(z)))
    delta[...] = step_size
    pairs = ((delta, delta_hbm), (inside_ref, inside_hbm), (before_ref, before_hbm), (pay_ref, pay_hbm))
    copies = [pltpu.make_async_copy(source, target, sems.at[i]) for i, (source, target) in enumerate(pairs)]
    copies[0].start()
    drive[...] = step_size * act_ref[...]
    b_all[...] = jnp.dot(g_ref[:, rank:], spread_ref[...], preferred_element_type=F32)
    chunk = lax.broadcasted_iota(jnp.int32, (CHUNKS, LANES), 0)
    zero = jnp.zeros((CHUNKS, LANES), F32)

    def add(step, totals):
        at = step_rows(step)
        totals = [totals[half] + delta[at, half * LANES : (half + 1) * LANES] for half in range(halves)]
        for half in range(halves):
            cum_ref[at, half * LANES : (half + 1) * LANES] = totals[half]
        return totals

    totals = lax.fori_loop(0, steps, add, [zero] * halves, unroll=8)
    for half in range(halves):
        cols = slice(half * LANES, (half + 1) * LANES)
        rates = [jnp.broadcast_to(rate[n : n + 1, cols], (CHUNKS, LANES)) for n in range(STATE)]
        total = totals[half]

        def gather(step, states, cols=cols, rates=rates, total=total):
            at = step_rows(step)
            left = total - cum_ref[at, cols]
            push = drive[at, cols]
            return [
                states[n] + jnp.exp2(left * rates[n]) * (push * b_all[at, n * LANES : (n + 1) * LANES])
                for n in range(STATE)
            ]

        states = lax.fori_loop(0, steps, gather, [zero] * STATE, unroll=8)
        sums = [total]
        shift = 1
        while shift < CHUNKS:
            sums.append(sums[-1] + jnp.where(chunk >= shift, pltpu.roll(sums[-1], shift, 0), 0.0))
            shift *= 2
        for n in range(STATE):
            end = states[n]
            shift = 1
            for level in range(len(sums) - 1):
                end = end + jnp.exp2(rates[n] * sums[level]) * jnp.where(
                    chunk >= shift, pltpu.roll(end, shift, 0), 0.0
                )
                shift *= 2
            inside_ref[n, :, cols] = jnp.where(chunk >= 1, pltpu.roll(end, 1, 0), 0.0)
            ends[n : n + 1, cols] = end[CHUNKS - 1 :, :]
        before_ref[:, cols] = jnp.where(chunk >= 1, pltpu.roll(sums[-1], 1, 0), 0.0)
        ends[STATE : STATE + 1, cols] = sums[-1][CHUNKS - 1 :, :]

    copies[1].start()
    copies[2].start()
    me = lax.axis_index("ctx")
    value = ends[0:STATE, :]
    total = jnp.broadcast_to(ends[STATE : STATE + 1, :], value.shape)
    high = total.astype(BF16).astype(F32)
    first = lax.broadcasted_iota(jnp.int32, value.shape, 0) == 0
    tail = jnp.where(first, high, total - high)
    for target in range(pay_ref.shape[0]):
        use = target > me
        pay_ref[target, 0:16, :] = jnp.where(use, value, 0.0).astype(BF16)
        pay_ref[target, 16:32, :] = jnp.where(use, tail, 0.0).astype(BF16)
    copies[3].start()
    for copy in copies:
        copy.wait()


def local_kernel(
    rank, g_ref, act_ref, rate, spread_ref, delta_hbm, inside_hbm, before_hbm, gain_hbm,
    y_ref, cum_ref, maps_ref,
    b_all, c_all, delta, inside_ref, before_ref, gain_ref, sems,
):
    rows, width = act_ref.shape
    steps = rows // CHUNKS
    halves = width // LANES
    pairs = ((delta_hbm, delta), (inside_hbm, inside_ref), (before_hbm, before_ref), (gain_hbm, gain_ref))
    copies = [pltpu.make_async_copy(source, target, sems.at[i]) for i, (source, target) in enumerate(pairs)]
    for copy in copies:
        copy.start()
    maps = g_ref[:, rank:]
    b_all[...] = jnp.dot(maps, spread_ref[...], preferred_element_type=F32)
    maps_ref[...] = pltpu.roll(maps.astype(F32), LANES - STATE, 1).astype(BF16)
    c_all[...] = jnp.dot(maps_ref[...], spread_ref[...], preferred_element_type=F32)
    for copy in copies:
        copy.wait()
    for half in range(halves):
        cols = slice(half * LANES, (half + 1) * LANES)
        rates = [jnp.broadcast_to(rate[n : n + 1, cols], (CHUNKS, LANES)) for n in range(STATE)]
        gain = gain_ref[:, cols]

        def advance(step, carried, cols=cols, rates=rates, gain=gain):
            states, total = carried
            at = step_rows(step)
            size = delta[at, cols]
            value = act_ref[at, cols]
            push = size * value
            total = total + size
            out = gain * value
            later = []
            for n in range(STATE):
                group = slice(n * LANES, (n + 1) * LANES)
                now = jnp.exp2(size * rates[n]) * states[n] + push * b_all[at, group]
                out = out + c_all[at, group] * now
                later.append(now)
            y_ref[at, cols] = out
            cum_ref[at, cols] = total
            return later, total

        lax.fori_loop(
            0, steps, advance, ([inside_ref[n, :, cols] for n in range(STATE)], before_ref[:, cols]), unroll=8
        )


def finish_kernel(got_ref, maps_ref, spread_ref, y_ref, cum_ref, rate, lit_ref, out_hbm, c_all, carry, ys, out_ref, sems):
    rows, width = y_ref.shape
    steps = rows // CHUNKS
    halves = width // LANES
    c_all[...] = jnp.dot(maps_ref[...], spread_ref[...], preferred_element_type=F32)
    incoming = jnp.zeros((STATE, width), F32)
    for source in range(got_ref.shape[0] - 1):
        tail = got_ref[source, 16:32, :].astype(F32)
        decay = jnp.exp2(rate[...] * (tail[0:1, :] + tail[1:2, :]))
        incoming = decay * incoming + got_ref[source, 0:16, :].astype(F32)
    carry[...] = incoming
    leaving = []
    for half in range(halves):
        cols = slice(half * LANES, (half + 1) * LANES)
        rates = [jnp.broadcast_to(rate[n : n + 1, cols], (CHUNKS, LANES)) for n in range(STATE)]
        entering = [jnp.broadcast_to(carry[n : n + 1, cols], (CHUNKS, LANES)) for n in range(STATE)]

        def correct(step, _, half=half, cols=cols, rates=rates, entering=entering):
            at = step_rows(step)
            total = cum_ref[at, cols]
            out = y_ref[at, cols]
            for n in range(STATE):
                group = slice(n * LANES, (n + 1) * LANES)
                out = out + (c_all[at, group] * entering[n]) * jnp.exp2(total * rates[n])
            ys[half, pl.ds(step, CHUNKS, stride=steps), :] = out
            return 0

        lax.fori_loop(0, steps, correct, 0, unroll=8)
        out_ref[half] = (ys[half] * lit_ref[:, cols]).astype(BF16)
        copy = pltpu.make_async_copy(out_ref.at[half], out_hbm.at[:, cols], sems.at[half])
        copy.start()
        leaving.append(copy)
    for copy in leaving:
        copy.wait()


def on_device(
    mamba_in, mamba_gate, conv_weight, conv_bias, proj_delta, proj_select, delta_weight, delta_bias, decay_log, skip_gain,
):
    rows, width = mamba_in.shape
    rank = proj_delta.shape[1]
    maps = proj_select.shape[1]
    halves = width // LANES
    steps = rows // CHUNKS
    n_ctx, n_ch = lax.axis_size("ctx"), lax.axis_size("ch")
    wide = rank + LANES
    cells = rows * width * STATE
    tile = jax.ShapeDtypeStruct((rows, width), F32)
    part_shape = jax.ShapeDtypeStruct((rows, wide), BF16)
    big = pltpu.VMEM((rows, STATE * LANES), F32)

    halo = lax.ppermute(mamba_in[rows - 16 :], "ctx", [(i, i + 1) for i in range(n_ctx - 1)])
    act, part, head, pd, sel, taps, dw, rate, vecs = pl.pallas_call(
        project_kernel,
        out_shape=(
            tile,
            part_shape,
            jax.ShapeDtypeStruct((8, width), F32),
            jax.ShapeDtypeStruct(proj_delta.shape, BF16),
            jax.ShapeDtypeStruct((LANES, width), BF16),
            jax.ShapeDtypeStruct((8, width), F32),
            jax.ShapeDtypeStruct(delta_weight.shape, BF16),
            jax.ShapeDtypeStruct((STATE, width), F32),
            jax.ShapeDtypeStruct((8, width), F32),
        ),
        in_specs=hbm(8),
        out_specs=tuple(vmem(9)),
        scratch_shapes=[
            pltpu.VMEM((rows, width), BF16),
            pltpu.VMEM((STATE, width), F32),
            pltpu.VMEM((KWIDTH, width), F32),
            pltpu.VMEM((1, width), F32),
            pltpu.VMEM((maps, width), BF16),
            pltpu.VMEM((halves, rows + 8, LANES), F32),
            pltpu.VMEM((halves, (steps + KWIDTH - 1) * CHUNKS, LANES), F32),
            pltpu.VMEM((rows, width), BF16),
            pltpu.SemaphoreType.DMA((8,)),
        ],
        compiler_params=pltpu.CompilerParams(vmem_limit_bytes=16 * MIB),
        cost_estimate=pl.CostEstimate(
            flops=2 * rows * width * wide, bytes_accessed=2 * rows * width * 8, transcendentals=rows * width
        ),
        name="project",
    )(
        *stay(
            mamba_in, proj_delta, proj_select.T, conv_weight, conv_bias[None, :],
            delta_weight, decay_log, delta_bias[None, :],
        )
    )
    act, part = pl.pallas_call(
        functools.partial(head_kernel, maps),
        out_shape=(tile, part_shape),
        in_specs=vmem(7),
        out_specs=tuple(vmem(2)),
        scratch_shapes=[pltpu.VMEM((16, width), F32)],
        compiler_params=pltpu.CompilerParams(vmem_limit_bytes=16 * MIB),
        name="first_rows",
    )(halo, head, taps, pd, sel, act, part)

    near = n_ch // 2
    groups = [list(range(near)), list(range(near, n_ch))]
    own = rows // near
    parts = lax.all_to_all(part.reshape(near, own, wide), "ch", 0, 0, axis_index_groups=groups)
    mine, send = pl.pallas_call(
        functools.partial(total_kernel, rank, maps),
        out_shape=(jax.ShapeDtypeStruct((own, wide), F32), jax.ShapeDtypeStruct((own, wide), BF16)),
        in_specs=vmem(1),
        out_specs=tuple(vmem(2)),
        compiler_params=pltpu.CompilerParams(vmem_limit_bytes=16 * MIB),
        name="total",
    )(parts)
    other = lax.ppermute(send, "ch", [(i, (i + near) % n_ch) for i in range(n_ch)])
    lit, spread, done = pl.pallas_call(
        ready_kernel,
        out_shape=(
            tile,
            jax.ShapeDtypeStruct((LANES, STATE * LANES), BF16),
            jax.ShapeDtypeStruct((8, LANES), F32),
        ),
        in_specs=vmem(1) + hbm(1),
        out_specs=tuple(vmem(3)),
        scratch_shapes=[pltpu.VMEM((rows, width), BF16), pltpu.SemaphoreType.DMA],
        compiler_params=pltpu.CompilerParams(vmem_limit_bytes=16 * MIB),
        cost_estimate=pl.CostEstimate(
            flops=16 * rows * width, bytes_accessed=8 * rows * width, transcendentals=rows * width
        ),
        name="ready",
    )(mine, *stay(mamba_gate))
    totals = pl.pallas_call(
        functools.partial(share_kernel, rank, maps),
        out_shape=jax.ShapeDtypeStruct(parts.shape, BF16),
        in_specs=vmem(3),
        out_specs=vmem(1)[0],
        compiler_params=pltpu.CompilerParams(vmem_limit_bytes=16 * MIB),
        name="share",
    )(mine, other, done)
    gathered = lax.all_to_all(totals, "ch", 0, 0, axis_index_groups=groups).reshape(rows, wide)

    sent = (
        ((rows, width), F32),
        ((STATE, CHUNKS, width), F32),
        ((CHUNKS, width), F32),
        ((n_ctx, 2 * STATE, width), BF16),
    )
    delta, inside, before, pay = pl.pallas_call(
        functools.partial(ends_kernel, rank),
        out_shape=tuple(pltpu.HBM(*kept) for kept in sent),
        in_specs=vmem(6),
        out_specs=tuple(hbm(4)),
        scratch_shapes=[
            *(pltpu.VMEM(*kept) for kept in sent),
            pltpu.VMEM((rows, width), F32),
            big,
            pltpu.VMEM((rows, width), F32),
            pltpu.VMEM((STATE + 8, width), F32),
            pltpu.SemaphoreType.DMA((4,)),
        ],
        compiler_params=pltpu.CompilerParams(vmem_limit_bytes=16 * MIB),
        name="ends",
    )(gathered, act, dw, vecs, rate, spread)

    got = lax.all_to_all(pay, "ctx", 0, 0)
    y_local, cum, maps_all = pl.pallas_call(
        functools.partial(local_kernel, rank),
        out_shape=(
            tile,
            tile,
            jax.ShapeDtypeStruct((rows, LANES), BF16),
        ),
        in_specs=vmem(4) + hbm(4),
        out_specs=tuple(vmem(3)),
        scratch_shapes=[
            big,
            big,
            *(pltpu.VMEM(*kept) for kept in sent[:3]),
            pltpu.VMEM((1, width), F32),
            pltpu.SemaphoreType.DMA((4,)),
        ],
        compiler_params=pltpu.CompilerParams(vmem_limit_bytes=24 * MIB),
        cost_estimate=pl.CostEstimate(flops=6 * cells, bytes_accessed=8 * rows * width * 4, transcendentals=cells),
        name="local_scan",
    )(gathered, act, rate, spread, *stay(delta, inside, before, skip_gain[None, :]))
    return pl.pallas_call(
        finish_kernel,
        out_shape=jax.ShapeDtypeStruct((rows, width), BF16),
        in_specs=vmem(7),
        out_specs=hbm(1)[0],
        scratch_shapes=[
            big,
            pltpu.VMEM((STATE, width), F32),
            pltpu.VMEM((halves, rows, LANES), F32),
            pltpu.VMEM((halves, rows, LANES), BF16),
            pltpu.SemaphoreType.DMA((halves,)),
        ],
        compiler_params=pltpu.CompilerParams(vmem_limit_bytes=16 * MIB),
        name="finish",
    )(got, maps_all, spread, y_local, cum, rate, lit)


def solution(mesh):
    return jax.shard_map(
        on_device,
        mesh=mesh,
        in_specs=(
            P("ctx", "ch"),
            P("ctx", "ch"),
            P(None, "ch"),
            P("ch"),
            P("ch", None),
            P("ch", None),
            P(None, "ch"),
            P("ch"),
            P(None, "ch"),
            P("ch"),
        ),
        out_specs=P("ctx", "ch"),
        check_vma=False,
    )
```

```python
import functools
import math

import jax
import jax.numpy as jnp
from jax import lax
from jax.experimental import pallas as pl
from jax.experimental.pallas import tpu as pltpu
from jax.sharding import PartitionSpec as P

STATE = 16
KWIDTH = 4
LANES = 128
CHUNKS = 8
OWN = 16
HEAD = 32
LOG2E = 1.0 / math.log(2.0)
MIB = 1 << 20
F32 = jnp.float32
BF16 = jnp.bfloat16


def vmem(count):
    return [pl.BlockSpec(memory_space=pltpu.VMEM)] * count


def hbm(count):
    return [pl.BlockSpec(memory_space=pltpu.HBM)] * count


def stay(*arrays):
    return [pltpu.with_memory_space_constraint(array, pltpu.HBM) for array in arrays]


def silu(value):
    return value / (1.0 + jnp.exp(-value))


def pack(low, first, second):
    pieces = [low[:, at : at + LANES] for at in range(0, low.shape[1], LANES)]
    return jnp.concatenate(pieces + [first + pltpu.roll(second, LANES // 2, 1)], axis=0).astype(BF16)


def put_products(low, pd, sel, maps, part_ref, products, chosen):
    rows = low.shape[0]
    products[0:rows, :] = jnp.dot(low, pd, preferred_element_type=F32)
    both = lax.dot_general(low, sel, (((1,), (1,)), ((), ())), preferred_element_type=F32)
    high = both.astype(BF16).astype(F32)
    lane = lax.broadcasted_iota(jnp.int32, both.shape, 1)
    chosen[0:rows, :] = jnp.where(lane < maps, high, both - high)
    for block in range(rows // OWN):
        at = block * OWN
        part_ref[block] = pack(
            products[at : at + OWN, :], chosen[at : at + OWN // 2, :], chosen[at + OWN // 2 : at + OWN, :]
        )


def project_kernel(
    x_hbm, pd_hbm, ps_hbm, weight_hbm, bias_hbm, dw_hbm, log_hbm, dbias_hbm,
    act_ref, part_ref, head_ref, pd_ref, sel_ref, taps_ref, dw_ref, rate_ref, vecs_ref,
    x_ref, log_ref, weight_ref, bias_ref, ps_ref, xs, xp, low, products, chosen, sems,
):
    rows, width = x_ref.shape
    steps = rows // CHUNKS
    maps = ps_ref.shape[0]
    halves = width // LANES
    pairs = (
        (x_hbm, x_ref), (weight_hbm, weight_ref), (bias_hbm, bias_ref), (ps_hbm, ps_ref), (pd_hbm, pd_ref),
        (log_hbm, log_ref), (dw_hbm, dw_ref), (dbias_hbm, vecs_ref.at[0:1]),
    )
    copies = [pltpu.make_async_copy(source, target, sems.at[i]) for i, (source, target) in enumerate(pairs)]
    for copy in copies:
        copy.start()
    copies[0].wait()
    head_ref[...] = x_ref[0:16, :].astype(F32)[0:8, :]
    for half in range(halves):
        cols = slice(half * LANES, (half + 1) * LANES)
        xs[half, 0:8, :] = jnp.zeros((8, LANES), F32)
        xs[half, 8 : 8 + rows, :] = x_ref[:, cols].astype(F32)
        for step in range(-(KWIDTH - 1), steps):
            to = (step + KWIDTH - 1) * CHUNKS
            xp[half, to : to + CHUNKS, :] = xs[half, pl.ds(8 + step, CHUNKS, stride=steps), :]
    copies[1].wait()
    copies[2].wait()
    taps_ref[0:KWIDTH, :] = weight_ref[...]
    taps_ref[KWIDTH : KWIDTH + 1, :] = bias_ref[...]
    block = min(rows, 64)
    for half in range(halves):
        cols = slice(half * LANES, (half + 1) * LANES)
        for start in range(0, rows, block):
            value = bias_ref[:, cols]
            for tap in range(KWIDTH):
                at = start + tap * CHUNKS
                value = value + weight_ref[tap : tap + 1, cols] * xp[half, at : at + block, :]
            value = silu(value)
            act_ref[start : start + block, cols] = value
            low[start : start + block, cols] = value.astype(BF16)
    copies[3].wait()
    sel_ref[...] = jnp.zeros_like(sel_ref)
    sel_ref[0:maps, :] = ps_ref[...]
    sel_ref[maps : 2 * maps, :] = ps_ref[...]
    copies[4].wait()
    put_products(low[...], pd_ref[...], sel_ref[...], maps, part_ref, products, chosen)
    copies[5].wait()
    rate_ref[...] = -jnp.exp(log_ref[...]) * LOG2E
    for copy in copies[6:]:
        copy.wait()


def head_kernel(maps, halo_ref, head_ref, taps_ref, pd_ref, sel_ref, act_in, part_in, act_ref, part_ref, ext, products, chosen):
    ext[0:8, :] = halo_ref[...].astype(F32)[-8:, :]
    ext[8:16, :] = head_ref[...]
    value = taps_ref[KWIDTH : KWIDTH + 1, :]
    for tap in range(KWIDTH):
        at = 8 - (KWIDTH - 1) + tap
        value = value + taps_ref[tap : tap + 1, :] * ext[at : at + 8, :]
    value = silu(value)
    act_ref[...] = act_in[...]
    part_ref[...] = part_in[...]
    for token in range(KWIDTH - 1):
        act_ref[token * CHUNKS : token * CHUNKS + 1, :] = value[token : token + 1, :]
    low = act_ref[0:HEAD, :].astype(BF16)
    put_products(low, pd_ref[...], sel_ref[...], maps, part_ref, products, chosen)


def fold(chosen, maps):
    lane = lax.broadcasted_iota(jnp.int32, chosen.shape, 1)
    summed = chosen + pltpu.roll(chosen, LANES - maps, 1)
    twice = jnp.where(lane < maps, summed, pltpu.roll(summed, maps, 1))
    return jnp.where(lane < 2 * maps, twice, 0.0)


def parted(twice, maps):
    lane = lax.broadcasted_iota(jnp.int32, twice.shape, 1)
    high = twice.astype(BF16).astype(F32)
    return jnp.where(lane < maps, high, twice - high)


def total_kernel(maps, parts_ref, mine_ref, send_ref):
    total = parts_ref[0].astype(F32)
    for source in range(1, parts_ref.shape[0]):
        total = total + parts_ref[source].astype(F32)
    cut = total.shape[0] - OWN // 2
    low, packed = total[:cut, :], total[cut:, :]
    twice = jnp.concatenate([fold(packed, maps), fold(pltpu.roll(packed, LANES // 2, 1), maps)], axis=0)
    mine_ref[...] = jnp.concatenate([low, twice], axis=0)
    send_ref[...] = jnp.concatenate([low, parted(twice, maps)], axis=0).astype(BF16)


def share_kernel(maps, mine_ref, other_ref, ready_ref, out_ref):
    cut = mine_ref.shape[0] - OWN
    other = other_ref[...].astype(F32)
    low = mine_ref[:cut, :] + other[:cut, :]
    twice = parted(mine_ref[cut:, :] + fold(other[cut:, :], maps), maps)
    packed = twice[: OWN // 2, :] + pltpu.roll(twice[OWN // 2 :, :], LANES // 2, 1)
    block = jnp.concatenate([low, packed], axis=0).astype(BF16)
    for target in range(out_ref.shape[0]):
        out_ref[target] = block


def ready_kernel(mine_ref, gate_hbm, lit_ref, spread_ref, done_ref, gate_ref, sem):
    copy = pltpu.make_async_copy(gate_hbm, gate_ref, sem)
    copy.start()
    source = lax.broadcasted_iota(jnp.int32, spread_ref.shape, 0)
    group = lax.broadcasted_iota(jnp.int32, spread_ref.shape, 1) >> 7
    hit = (source == group) | (source == group + 2 * STATE)
    spread_ref[...] = jnp.where(hit, 1.0, 0.0).astype(BF16)
    done_ref[...] = jnp.zeros_like(done_ref)
    copy.wait()
    lit_ref[...] = silu(gate_ref[...].astype(F32))


def step_rows(step):
    return pl.ds(pl.multiple_of(step * CHUNKS, CHUNKS), CHUNKS)


def ends_kernel(
    g_ref, act_ref, dw_ref, vecs_ref, rate, spread_ref,
    delta_hbm, inside_hbm, before_hbm, maps_hbm, pay_hbm,
    delta, inside_ref, before_ref, maps_ref, pay_ref, low, drive, b_all, cum_ref, ends, sems,
):
    rows, width = act_ref.shape
    steps = rows // CHUNKS
    halves = width // LANES
    for block in range(g_ref.shape[0]):
        at = slice(block * OWN, (block + 1) * OWN)
        for piece in range(low.shape[1] // LANES):
            low[at, piece * LANES : (piece + 1) * LANES] = g_ref[block, piece * OWN : (piece + 1) * OWN, :]
        packed = g_ref[block].astype(F32)[-(OWN // 2) :, :]
        maps_ref[at, :] = jnp.concatenate([packed, pltpu.roll(packed, LANES // 2, 1)], axis=0).astype(BF16)
    z = jnp.dot(low[...], dw_ref[...], preferred_element_type=F32) + vecs_ref[0:1, :]
    step_size = jnp.maximum(z, 0.0) + jnp.log1p(jnp.exp(-jnp.abs(z)))
    delta[...] = step_size
    pairs = (
        (delta, delta_hbm), (maps_ref, maps_hbm),
        (inside_ref, inside_hbm), (before_ref, before_hbm), (pay_ref, pay_hbm),
    )
    copies = [pltpu.make_async_copy(source, target, sems.at[i]) for i, (source, target) in enumerate(pairs)]
    copies[0].start()
    copies[1].start()
    drive[...] = step_size * act_ref[...]
    b_all[...] = jnp.dot(maps_ref[...], spread_ref[...], preferred_element_type=F32)
    chunk = lax.broadcasted_iota(jnp.int32, (CHUNKS, LANES), 0)
    zero = jnp.zeros((CHUNKS, LANES), F32)

    def add(step, totals):
        at = step_rows(step)
        totals = [totals[half] + delta[at, half * LANES : (half + 1) * LANES] for half in range(halves)]
        for half in range(halves):
            cum_ref[at, half * LANES : (half + 1) * LANES] = totals[half]
        return totals

    totals = lax.fori_loop(0, steps, add, [zero] * halves, unroll=8)
    for half in range(halves):
        cols = slice(half * LANES, (half + 1) * LANES)
        rates = [jnp.broadcast_to(rate[n : n + 1, cols], (CHUNKS, LANES)) for n in range(STATE)]
        total = totals[half]

        def gather(step, states, cols=cols, rates=rates, total=total):
            at = step_rows(step)
            left = total - cum_ref[at, cols]
            push = drive[at, cols]
            return [
                states[n] + jnp.exp2(left * rates[n]) * (push * b_all[at, n * LANES : (n + 1) * LANES])
                for n in range(STATE)
            ]

        states = lax.fori_loop(0, steps, gather, [zero] * STATE, unroll=8)
        sums = [total]
        shift = 1
        while shift < CHUNKS:
            sums.append(sums[-1] + jnp.where(chunk >= shift, pltpu.roll(sums[-1], shift, 0), 0.0))
            shift *= 2
        for n in range(STATE):
            end = states[n]
            shift = 1
            for level in range(len(sums) - 1):
                end = end + jnp.exp2(rates[n] * sums[level]) * jnp.where(
                    chunk >= shift, pltpu.roll(end, shift, 0), 0.0
                )
                shift *= 2
            inside_ref[n, :, cols] = jnp.where(chunk >= 1, pltpu.roll(end, 1, 0), 0.0)
            ends[n : n + 1, cols] = end[CHUNKS - 1 :, :]
        before_ref[:, cols] = jnp.where(chunk >= 1, pltpu.roll(sums[-1], 1, 0), 0.0)
        ends[STATE : STATE + 1, cols] = sums[-1][CHUNKS - 1 :, :]

    copies[2].start()
    copies[3].start()
    me = lax.axis_index("ctx")
    value = ends[0:STATE, :]
    total = jnp.broadcast_to(ends[STATE : STATE + 1, :], value.shape)
    high = total.astype(BF16).astype(F32)
    first = lax.broadcasted_iota(jnp.int32, value.shape, 0) == 0
    tail = jnp.where(first, high, total - high)
    for target in range(pay_ref.shape[0]):
        use = target > me
        pay_ref[target, 0:16, :] = jnp.where(use, value, 0.0).astype(BF16)
        pay_ref[target, 16:32, :] = jnp.where(use, tail, 0.0).astype(BF16)
    copies[4].start()
    for copy in copies:
        copy.wait()


def local_kernel(
    act_ref, rate, spread_ref, delta_hbm, inside_hbm, before_hbm, maps_hbm, gain_hbm,
    y_ref, cum_ref, maps_ref,
    b_all, c_all, delta, inside_ref, before_ref, both_ref, gain_ref, sems,
):
    rows, width = act_ref.shape
    steps = rows // CHUNKS
    halves = width // LANES
    pairs = (
        (maps_hbm, both_ref), (delta_hbm, delta),
        (inside_hbm, inside_ref), (before_hbm, before_ref), (gain_hbm, gain_ref),
    )
    copies = [pltpu.make_async_copy(source, target, sems.at[i]) for i, (source, target) in enumerate(pairs)]
    for copy in copies:
        copy.start()
    copies[0].wait()
    maps = both_ref[...]
    b_all[...] = jnp.dot(maps, spread_ref[...], preferred_element_type=F32)
    maps_ref[...] = pltpu.roll(maps.astype(F32), LANES - STATE, 1).astype(BF16)
    c_all[...] = jnp.dot(maps_ref[...], spread_ref[...], preferred_element_type=F32)
    for copy in copies[1:]:
        copy.wait()
    for half in range(halves):
        cols = slice(half * LANES, (half + 1) * LANES)
        rates = [jnp.broadcast_to(rate[n : n + 1, cols], (CHUNKS, LANES)) for n in range(STATE)]
        gain = gain_ref[:, cols]

        def advance(step, carried, cols=cols, rates=rates, gain=gain):
            states, total = carried
            at = step_rows(step)
            size = delta[at, cols]
            value = act_ref[at, cols]
            push = size * value
            total = total + size
            out = gain * value
            later = []
            for n in range(STATE):
                group = slice(n * LANES, (n + 1) * LANES)
                now = jnp.exp2(size * rates[n]) * states[n] + push * b_all[at, group]
                out = out + c_all[at, group] * now
                later.append(now)
            y_ref[at, cols] = out
            cum_ref[at, cols] = total
            return later, total

        lax.fori_loop(
            0, steps, advance, ([inside_ref[n, :, cols] for n in range(STATE)], before_ref[:, cols]), unroll=8
        )


def finish_kernel(got_ref, maps_ref, spread_ref, y_ref, cum_ref, rate, lit_ref, out_hbm, c_all, carry, ys, out_ref, sems):
    rows, width = y_ref.shape
    steps = rows // CHUNKS
    halves = width // LANES
    c_all[...] = jnp.dot(maps_ref[...], spread_ref[...], preferred_element_type=F32)
    incoming = jnp.zeros((STATE, width), F32)
    for source in range(got_ref.shape[0] - 1):
        tail = got_ref[source, 16:32, :].astype(F32)
        decay = jnp.exp2(rate[...] * (tail[0:1, :] + tail[1:2, :]))
        incoming = decay * incoming + got_ref[source, 0:16, :].astype(F32)
    carry[...] = incoming
    leaving = []
    for half in range(halves):
        cols = slice(half * LANES, (half + 1) * LANES)
        rates = [jnp.broadcast_to(rate[n : n + 1, cols], (CHUNKS, LANES)) for n in range(STATE)]
        entering = [jnp.broadcast_to(carry[n : n + 1, cols], (CHUNKS, LANES)) for n in range(STATE)]

        def correct(step, _, half=half, cols=cols, rates=rates, entering=entering):
            at = step_rows(step)
            total = cum_ref[at, cols]
            out = y_ref[at, cols]
            for n in range(STATE):
                group = slice(n * LANES, (n + 1) * LANES)
                out = out + (c_all[at, group] * entering[n]) * jnp.exp2(total * rates[n])
            ys[half, pl.ds(step, CHUNKS, stride=steps), :] = out
            return 0

        lax.fori_loop(0, steps, correct, 0, unroll=8)
        out_ref[half] = (ys[half] * lit_ref[:, cols]).astype(BF16)
        copy = pltpu.make_async_copy(out_ref.at[half], out_hbm.at[:, cols], sems.at[half])
        copy.start()
        leaving.append(copy)
    for copy in leaving:
        copy.wait()


def on_device(
    mamba_in, mamba_gate, conv_weight, conv_bias, proj_delta, proj_select, delta_weight, delta_bias, decay_log, skip_gain,
):
    rows, width = mamba_in.shape
    rank = proj_delta.shape[1]
    maps = proj_select.shape[1]
    halves = width // LANES
    steps = rows // CHUNKS
    n_ctx, n_ch = lax.axis_size("ctx"), lax.axis_size("ch")
    wide = rank + LANES
    cells = rows * width * STATE
    tile = jax.ShapeDtypeStruct((rows, width), F32)
    near = n_ch // 2
    tall = OWN * rank // LANES + OWN // 2
    part_shape = jax.ShapeDtypeStruct((near, tall, LANES), BF16)
    big = pltpu.VMEM((rows, STATE * LANES), F32)

    halo = lax.ppermute(mamba_in[rows - 16 :], "ctx", [(i, i + 1) for i in range(n_ctx - 1)])
    act, part, head, pd, sel, taps, dw, rate, vecs = pl.pallas_call(
        project_kernel,
        out_shape=(
            tile,
            part_shape,
            jax.ShapeDtypeStruct((8, width), F32),
            jax.ShapeDtypeStruct(proj_delta.shape, BF16),
            jax.ShapeDtypeStruct((LANES, width), BF16),
            jax.ShapeDtypeStruct((8, width), F32),
            jax.ShapeDtypeStruct(delta_weight.shape, BF16),
            jax.ShapeDtypeStruct((STATE, width), F32),
            jax.ShapeDtypeStruct((8, width), F32),
        ),
        in_specs=hbm(8),
        out_specs=tuple(vmem(9)),
        scratch_shapes=[
            pltpu.VMEM((rows, width), BF16),
            pltpu.VMEM((STATE, width), F32),
            pltpu.VMEM((KWIDTH, width), F32),
            pltpu.VMEM((1, width), F32),
            pltpu.VMEM((maps, width), BF16),
            pltpu.VMEM((halves, rows + 8, LANES), F32),
            pltpu.VMEM((halves, (steps + KWIDTH - 1) * CHUNKS, LANES), F32),
            pltpu.VMEM((rows, width), BF16),
            pltpu.VMEM((rows, rank), F32),
            pltpu.VMEM((rows, LANES), F32),
            pltpu.SemaphoreType.DMA((8,)),
        ],
        compiler_params=pltpu.CompilerParams(vmem_limit_bytes=16 * MIB),
        cost_estimate=pl.CostEstimate(
            flops=2 * rows * width * wide, bytes_accessed=2 * rows * width * 8, transcendentals=rows * width
        ),
        name="project",
    )(
        *stay(
            mamba_in, proj_delta, proj_select.T, conv_weight, conv_bias[None, :],
            delta_weight, decay_log, delta_bias[None, :],
        )
    )
    act, part = pl.pallas_call(
        functools.partial(head_kernel, maps),
        out_shape=(tile, part_shape),
        in_specs=vmem(7),
        out_specs=tuple(vmem(2)),
        scratch_shapes=[
            pltpu.VMEM((16, width), F32),
            pltpu.VMEM((HEAD, rank), F32),
            pltpu.VMEM((HEAD, LANES), F32),
        ],
        compiler_params=pltpu.CompilerParams(vmem_limit_bytes=16 * MIB),
        name="first_rows",
    )(halo, head, taps, pd, sel, act, part)

    groups = [list(range(near)), list(range(near, n_ch))]
    parts = lax.all_to_all(part, "ch", 0, 0, axis_index_groups=groups)
    mine, send = pl.pallas_call(
        functools.partial(total_kernel, maps),
        out_shape=tuple(jax.ShapeDtypeStruct((tall + OWN // 2, LANES), kind) for kind in (F32, BF16)),
        in_specs=vmem(1),
        out_specs=tuple(vmem(2)),
        compiler_params=pltpu.CompilerParams(vmem_limit_bytes=16 * MIB),
        name="total",
    )(parts)
    other = lax.ppermute(send, "ch", [(i, (i + near) % n_ch) for i in range(n_ch)])
    lit, spread, done = pl.pallas_call(
        ready_kernel,
        out_shape=(
            tile,
            jax.ShapeDtypeStruct((LANES, STATE * LANES), BF16),
            jax.ShapeDtypeStruct((8, LANES), F32),
        ),
        in_specs=vmem(1) + hbm(1),
        out_specs=tuple(vmem(3)),
        scratch_shapes=[pltpu.VMEM((rows, width), BF16), pltpu.SemaphoreType.DMA],
        compiler_params=pltpu.CompilerParams(vmem_limit_bytes=16 * MIB),
        cost_estimate=pl.CostEstimate(
            flops=16 * rows * width, bytes_accessed=8 * rows * width, transcendentals=rows * width
        ),
        name="ready",
    )(mine, *stay(mamba_gate))
    totals = pl.pallas_call(
        functools.partial(share_kernel, maps),
        out_shape=jax.ShapeDtypeStruct(parts.shape, BF16),
        in_specs=vmem(3),
        out_specs=vmem(1)[0],
        compiler_params=pltpu.CompilerParams(vmem_limit_bytes=16 * MIB),
        name="share",
    )(mine, other, done)
    gathered = lax.all_to_all(totals, "ch", 0, 0, axis_index_groups=groups)

    sent = (
        ((rows, width), F32),
        ((STATE, CHUNKS, width), F32),
        ((CHUNKS, width), F32),
        ((rows, LANES), BF16),
        ((n_ctx, 2 * STATE, width), BF16),
    )
    delta, inside, before, maps_all, pay = pl.pallas_call(
        ends_kernel,
        out_shape=tuple(pltpu.HBM(*kept) for kept in sent),
        in_specs=vmem(6),
        out_specs=tuple(hbm(5)),
        scratch_shapes=[
            *(pltpu.VMEM(*kept) for kept in sent),
            pltpu.VMEM((rows, rank), BF16),
            pltpu.VMEM((rows, width), F32),
            big,
            pltpu.VMEM((rows, width), F32),
            pltpu.VMEM((STATE + 8, width), F32),
            pltpu.SemaphoreType.DMA((5,)),
        ],
        compiler_params=pltpu.CompilerParams(vmem_limit_bytes=16 * MIB),
        name="ends",
    )(gathered, act, dw, vecs, rate, spread)

    got = lax.all_to_all(pay, "ctx", 0, 0)
    y_local, cum, turned = pl.pallas_call(
        local_kernel,
        out_shape=(
            tile,
            tile,
            jax.ShapeDtypeStruct((rows, LANES), BF16),
        ),
        in_specs=vmem(3) + hbm(5),
        out_specs=tuple(vmem(3)),
        scratch_shapes=[
            big,
            big,
            *(pltpu.VMEM(*kept) for kept in sent[:4]),
            pltpu.VMEM((1, width), F32),
            pltpu.SemaphoreType.DMA((5,)),
        ],
        compiler_params=pltpu.CompilerParams(vmem_limit_bytes=24 * MIB),
        cost_estimate=pl.CostEstimate(flops=6 * cells, bytes_accessed=8 * rows * width * 4, transcendentals=cells),
        name="local_scan",
    )(act, rate, spread, *stay(delta, inside, before, maps_all, skip_gain[None, :]))
    return pl.pallas_call(
        finish_kernel,
        out_shape=jax.ShapeDtypeStruct((rows, width), BF16),
        in_specs=vmem(7),
        out_specs=hbm(1)[0],
        scratch_shapes=[
            big,
            pltpu.VMEM((STATE, width), F32),
            pltpu.VMEM((halves, rows, LANES), F32),
            pltpu.VMEM((halves, rows, LANES), BF16),
            pltpu.SemaphoreType.DMA((halves,)),
        ],
        compiler_params=pltpu.CompilerParams(vmem_limit_bytes=16 * MIB),
        name="finish",
    )(got, turned, spread, y_local, cum, rate, lit)


def solution(mesh):
    return jax.shard_map(
        on_device,
        mesh=mesh,
        in_specs=(
            P("ctx", "ch"),
            P("ctx", "ch"),
            P(None, "ch"),
            P("ch"),
            P("ch", None),
            P("ch", None),
            P(None, "ch"),
            P("ch"),
            P(None, "ch"),
            P("ch"),
        ),
        out_specs=P("ctx", "ch"),
        check_vma=False,
    )
```

```python
import functools
import math

import jax
import jax.numpy as jnp
from jax import lax
from jax.experimental import pallas as pl
from jax.experimental.pallas import tpu as pltpu
from jax.sharding import PartitionSpec as P

STATE = 16
KWIDTH = 4
LANES = 128
CHUNKS = 8
OWN = 16
HEAD = 32
LOG2E = 1.0 / math.log(2.0)
MIB = 1 << 20
F32 = jnp.float32
BF16 = jnp.bfloat16


def vmem(count):
    return [pl.BlockSpec(memory_space=pltpu.VMEM)] * count


def hbm(count):
    return [pl.BlockSpec(memory_space=pltpu.HBM)] * count


def stay(*arrays):
    return [pltpu.with_memory_space_constraint(array, pltpu.HBM) for array in arrays]


def silu(value):
    return value / (1.0 + jnp.exp(-value))


def pack(low, first, second):
    pieces = [low[:, at : at + LANES] for at in range(0, low.shape[1], LANES)]
    return jnp.concatenate(pieces + [first + pltpu.roll(second, LANES // 2, 1)], axis=0).astype(BF16)


def put_products(low, pd, sel, maps, part_ref, products, chosen):
    rows = low.shape[0]
    products[0:rows, :] = jnp.dot(low, pd, preferred_element_type=F32)
    both = lax.dot_general(low, sel, (((1,), (1,)), ((), ())), preferred_element_type=F32)
    high = both.astype(BF16).astype(F32)
    lane = lax.broadcasted_iota(jnp.int32, both.shape, 1)
    chosen[0:rows, :] = jnp.where(lane < maps, high, both - high)
    for block in range(rows // OWN):
        at = block * OWN
        part_ref[block] = pack(
            products[at : at + OWN, :], chosen[at : at + OWN // 2, :], chosen[at + OWN // 2 : at + OWN, :]
        )


def project_kernel(
    x_hbm, pd_hbm, ps_hbm, weight_hbm, bias_hbm,
    act_ref, part_ref, head_ref, pd_ref, sel_ref, taps_ref,
    x_ref, weight_ref, bias_ref, ps_ref, xs, xp, low, products, chosen, sems,
):
    rows, width = x_ref.shape
    steps = rows // CHUNKS
    maps = ps_ref.shape[0]
    halves = width // LANES
    pairs = (
        (x_hbm, x_ref), (weight_hbm, weight_ref), (bias_hbm, bias_ref), (ps_hbm, ps_ref), (pd_hbm, pd_ref),
    )
    copies = [pltpu.make_async_copy(source, target, sems.at[i]) for i, (source, target) in enumerate(pairs)]
    for copy in copies:
        copy.start()
    copies[0].wait()
    head_ref[...] = x_ref[0:16, :].astype(F32)[0:8, :]
    for half in range(halves):
        cols = slice(half * LANES, (half + 1) * LANES)
        xs[half, 0:8, :] = jnp.zeros((8, LANES), F32)
        xs[half, 8 : 8 + rows, :] = x_ref[:, cols].astype(F32)
        for step in range(-(KWIDTH - 1), steps):
            to = (step + KWIDTH - 1) * CHUNKS
            xp[half, to : to + CHUNKS, :] = xs[half, pl.ds(8 + step, CHUNKS, stride=steps), :]
    copies[1].wait()
    copies[2].wait()
    taps_ref[0:KWIDTH, :] = weight_ref[...]
    taps_ref[KWIDTH : KWIDTH + 1, :] = bias_ref[...]
    block = min(rows, 64)
    for half in range(halves):
        cols = slice(half * LANES, (half + 1) * LANES)
        for start in range(0, rows, block):
            value = bias_ref[:, cols]
            for tap in range(KWIDTH):
                at = start + tap * CHUNKS
                value = value + weight_ref[tap : tap + 1, cols] * xp[half, at : at + block, :]
            value = silu(value)
            act_ref[start : start + block, cols] = value
            low[start : start + block, cols] = value.astype(BF16)
    copies[3].wait()
    sel_ref[...] = jnp.zeros_like(sel_ref)
    sel_ref[0:maps, :] = ps_ref[...]
    sel_ref[maps : 2 * maps, :] = ps_ref[...]
    copies[4].wait()
    put_products(low[...], pd_ref[...], sel_ref[...], maps, part_ref, products, chosen)


def head_kernel(maps, halo_ref, head_ref, taps_ref, pd_ref, sel_ref, act_in, part_in, act_ref, part_ref, ext, products, chosen):
    ext[0:8, :] = halo_ref[...].astype(F32)[-8:, :]
    ext[8:16, :] = head_ref[...]
    value = taps_ref[KWIDTH : KWIDTH + 1, :]
    for tap in range(KWIDTH):
        at = 8 - (KWIDTH - 1) + tap
        value = value + taps_ref[tap : tap + 1, :] * ext[at : at + 8, :]
    value = silu(value)
    act_ref[...] = act_in[...]
    part_ref[...] = part_in[...]
    for token in range(KWIDTH - 1):
        act_ref[token * CHUNKS : token * CHUNKS + 1, :] = value[token : token + 1, :]
    low = act_ref[0:HEAD, :].astype(BF16)
    put_products(low, pd_ref[...], sel_ref[...], maps, part_ref, products, chosen)


def fold(chosen, maps):
    lane = lax.broadcasted_iota(jnp.int32, chosen.shape, 1)
    summed = chosen + pltpu.roll(chosen, LANES - maps, 1)
    twice = jnp.where(lane < maps, summed, pltpu.roll(summed, maps, 1))
    return jnp.where(lane < 2 * maps, twice, 0.0)


def parted(twice, maps):
    lane = lax.broadcasted_iota(jnp.int32, twice.shape, 1)
    high = twice.astype(BF16).astype(F32)
    return jnp.where(lane < maps, high, twice - high)


def total_kernel(maps, parts_ref, mine_ref, send_ref):
    total = parts_ref[0].astype(F32)
    for source in range(1, parts_ref.shape[0]):
        total = total + parts_ref[source].astype(F32)
    cut = total.shape[0] - OWN // 2
    low, packed = total[:cut, :], total[cut:, :]
    twice = jnp.concatenate([fold(packed, maps), fold(pltpu.roll(packed, LANES // 2, 1), maps)], axis=0)
    mine_ref[...] = jnp.concatenate([low, twice], axis=0)
    send_ref[...] = jnp.concatenate([low, parted(twice, maps)], axis=0).astype(BF16)


def share_kernel(maps, mine_ref, other_ref, ready_ref, out_ref):
    cut = mine_ref.shape[0] - OWN
    other = other_ref[...].astype(F32)
    low = mine_ref[:cut, :] + other[:cut, :]
    twice = parted(mine_ref[cut:, :] + fold(other[cut:, :], maps), maps)
    packed = twice[: OWN // 2, :] + pltpu.roll(twice[OWN // 2 :, :], LANES // 2, 1)
    block = jnp.concatenate([low, packed], axis=0).astype(BF16)
    for target in range(out_ref.shape[0]):
        out_ref[target] = block


def ready_kernel(
    mine_ref, gate_hbm, dw_hbm, log_hbm, bias_hbm,
    lit_ref, spread_ref, done_ref, dw_ref, rate_ref, bias_ref,
    gate_ref, log_ref, sems,
):
    pairs = ((gate_hbm, gate_ref), (dw_hbm, dw_ref), (log_hbm, log_ref), (bias_hbm, bias_ref.at[0:1]))
    copies = [pltpu.make_async_copy(source, target, sems.at[i]) for i, (source, target) in enumerate(pairs)]
    for copy in copies:
        copy.start()
    source = lax.broadcasted_iota(jnp.int32, spread_ref.shape, 0)
    group = lax.broadcasted_iota(jnp.int32, spread_ref.shape, 1) >> 7
    hit = (source == group) | (source == group + 2 * STATE)
    spread_ref[...] = jnp.where(hit, 1.0, 0.0).astype(BF16)
    done_ref[...] = jnp.zeros_like(done_ref)
    for copy in copies:
        copy.wait()
    rate_ref[...] = -jnp.exp(log_ref[...]) * LOG2E
    lit_ref[...] = silu(gate_ref[...].astype(F32))


def step_rows(step):
    return pl.ds(pl.multiple_of(step * CHUNKS, CHUNKS), CHUNKS)


def ends_kernel(
    g_ref, act_ref, dw_ref, vecs_ref, rate, spread_ref,
    delta_hbm, inside_hbm, before_hbm, maps_hbm, pay_hbm,
    delta, inside_ref, before_ref, maps_ref, pay_ref, low, drive, b_all, cum_ref, ends, sems,
):
    rows, width = act_ref.shape
    steps = rows // CHUNKS
    halves = width // LANES
    for block in range(g_ref.shape[0]):
        at = slice(block * OWN, (block + 1) * OWN)
        for piece in range(low.shape[1] // LANES):
            low[at, piece * LANES : (piece + 1) * LANES] = g_ref[block, piece * OWN : (piece + 1) * OWN, :]
        packed = g_ref[block].astype(F32)[-(OWN // 2) :, :]
        maps_ref[at, :] = jnp.concatenate([packed, pltpu.roll(packed, LANES // 2, 1)], axis=0).astype(BF16)
    z = jnp.dot(low[...], dw_ref[...], preferred_element_type=F32) + vecs_ref[0:1, :]
    step_size = jnp.maximum(z, 0.0) + jnp.log1p(jnp.exp(-jnp.abs(z)))
    delta[...] = step_size
    pairs = (
        (delta, delta_hbm), (maps_ref, maps_hbm),
        (inside_ref, inside_hbm), (before_ref, before_hbm), (pay_ref, pay_hbm),
    )
    copies = [pltpu.make_async_copy(source, target, sems.at[i]) for i, (source, target) in enumerate(pairs)]
    copies[0].start()
    copies[1].start()
    drive[...] = step_size * act_ref[...]
    b_all[...] = jnp.dot(maps_ref[...], spread_ref[...], preferred_element_type=F32)
    chunk = lax.broadcasted_iota(jnp.int32, (CHUNKS, LANES), 0)
    zero = jnp.zeros((CHUNKS, LANES), F32)

    def add(step, totals):
        at = step_rows(step)
        totals = [totals[half] + delta[at, half * LANES : (half + 1) * LANES] for half in range(halves)]
        for half in range(halves):
            cum_ref[at, half * LANES : (half + 1) * LANES] = totals[half]
        return totals

    totals = lax.fori_loop(0, steps, add, [zero] * halves, unroll=8)
    for half in range(halves):
        cols = slice(half * LANES, (half + 1) * LANES)
        rates = [jnp.broadcast_to(rate[n : n + 1, cols], (CHUNKS, LANES)) for n in range(STATE)]
        total = totals[half]

        def gather(step, states, cols=cols, rates=rates, total=total):
            at = step_rows(step)
            left = total - cum_ref[at, cols]
            push = drive[at, cols]
            return [
                states[n] + jnp.exp2(left * rates[n]) * (push * b_all[at, n * LANES : (n + 1) * LANES])
                for n in range(STATE)
            ]

        states = lax.fori_loop(0, steps, gather, [zero] * STATE, unroll=16)
        sums = [total]
        shift = 1
        while shift < CHUNKS:
            sums.append(sums[-1] + jnp.where(chunk >= shift, pltpu.roll(sums[-1], shift, 0), 0.0))
            shift *= 2
        for n in range(STATE):
            end = states[n]
            shift = 1
            for level in range(len(sums) - 1):
                end = end + jnp.exp2(rates[n] * sums[level]) * jnp.where(
                    chunk >= shift, pltpu.roll(end, shift, 0), 0.0
                )
                shift *= 2
            inside_ref[n, :, cols] = jnp.where(chunk >= 1, pltpu.roll(end, 1, 0), 0.0)
            ends[n : n + 1, cols] = end[CHUNKS - 1 :, :]
        before_ref[:, cols] = jnp.where(chunk >= 1, pltpu.roll(sums[-1], 1, 0), 0.0)
        ends[STATE : STATE + 1, cols] = sums[-1][CHUNKS - 1 :, :]

    copies[2].start()
    copies[3].start()
    me = lax.axis_index("ctx")
    row = lax.broadcasted_iota(jnp.int32, (CHUNKS, LANES), 0)
    pieces, tail = [], zero
    for half in range(halves):
        cols = slice(half * LANES, (half + 1) * LANES)
        pieces.append(ends[0:STATE, cols])
        total = jnp.broadcast_to(ends[STATE : STATE + 1, cols], tail.shape)
        high = total.astype(BF16).astype(F32)
        tail = jnp.where(row == 2 * half, high, jnp.where(row == 2 * half + 1, total - high, tail))
    block = jnp.concatenate(pieces + [tail], axis=0)
    for target in range(pay_ref.shape[0]):
        pay_ref[target] = jnp.where(target > me, block, 0.0).astype(BF16)
    copies[4].start()
    for copy in copies:
        copy.wait()


def local_kernel(
    act_ref, rate, spread_ref, delta_hbm, inside_hbm, before_hbm, maps_hbm, gain_hbm,
    y_ref, cum_ref, maps_ref,
    b_all, c_all, delta, inside_ref, before_ref, both_ref, gain_ref, sems,
):
    rows, width = act_ref.shape
    steps = rows // CHUNKS
    halves = width // LANES
    pairs = (
        (maps_hbm, both_ref), (delta_hbm, delta),
        (inside_hbm, inside_ref), (before_hbm, before_ref), (gain_hbm, gain_ref),
    )
    copies = [pltpu.make_async_copy(source, target, sems.at[i]) for i, (source, target) in enumerate(pairs)]
    for copy in copies:
        copy.start()
    copies[0].wait()
    maps = both_ref[...]
    b_all[...] = jnp.dot(maps, spread_ref[...], preferred_element_type=F32)
    maps_ref[...] = pltpu.roll(maps.astype(F32), LANES - STATE, 1).astype(BF16)
    c_all[...] = jnp.dot(maps_ref[...], spread_ref[...], preferred_element_type=F32)
    for copy in copies[1:]:
        copy.wait()
    for half in range(halves):
        cols = slice(half * LANES, (half + 1) * LANES)
        rates = [jnp.broadcast_to(rate[n : n + 1, cols], (CHUNKS, LANES)) for n in range(STATE)]
        gain = gain_ref[:, cols]

        def advance(step, carried, cols=cols, rates=rates, gain=gain):
            states, total = carried
            at = step_rows(step)
            size = delta[at, cols]
            value = act_ref[at, cols]
            push = size * value
            total = total + size
            out = gain * value
            later = []
            for n in range(STATE):
                group = slice(n * LANES, (n + 1) * LANES)
                now = jnp.exp2(size * rates[n]) * states[n] + push * b_all[at, group]
                out = out + c_all[at, group] * now
                later.append(now)
            y_ref[at, cols] = out
            cum_ref[at, cols] = total
            return later, total

        lax.fori_loop(
            0, steps, advance, ([inside_ref[n, :, cols] for n in range(STATE)], before_ref[:, cols]), unroll=8
        )


def finish_kernel(got_ref, maps_ref, spread_ref, y_ref, cum_ref, rate, lit_ref, out_hbm, c_all, carry, ys, out_ref, sems):
    rows, width = y_ref.shape
    steps = rows // CHUNKS
    halves = width // LANES
    c_all[...] = jnp.dot(maps_ref[...], spread_ref[...], preferred_element_type=F32)
    incoming = [jnp.zeros((STATE, LANES), F32)] * halves
    for source in range(got_ref.shape[0] - 1):
        block = got_ref[source].astype(F32)
        tail = block[halves * STATE :, :]
        for half in range(halves):
            total = tail[2 * half : 2 * half + 1, :] + tail[2 * half + 1 : 2 * half + 2, :]
            decay = jnp.exp2(rate[:, half * LANES : (half + 1) * LANES] * total)
            incoming[half] = decay * incoming[half] + block[half * STATE : (half + 1) * STATE, :]
    for half in range(halves):
        carry[:, half * LANES : (half + 1) * LANES] = incoming[half]
    leaving = []
    for half in range(halves):
        cols = slice(half * LANES, (half + 1) * LANES)
        rates = [jnp.broadcast_to(rate[n : n + 1, cols], (CHUNKS, LANES)) for n in range(STATE)]
        entering = [jnp.broadcast_to(carry[n : n + 1, cols], (CHUNKS, LANES)) for n in range(STATE)]

        def correct(step, _, half=half, cols=cols, rates=rates, entering=entering):
            at = step_rows(step)
            total = cum_ref[at, cols]
            out = y_ref[at, cols]
            for n in range(STATE):
                group = slice(n * LANES, (n + 1) * LANES)
                out = out + (c_all[at, group] * entering[n]) * jnp.exp2(total * rates[n])
            ys[half, pl.ds(step, CHUNKS, stride=steps), :] = out
            return 0

        lax.fori_loop(0, steps, correct, 0, unroll=16)
        out_ref[half] = (ys[half] * lit_ref[:, cols]).astype(BF16)
        copy = pltpu.make_async_copy(out_ref.at[half], out_hbm.at[:, cols], sems.at[half])
        copy.start()
        leaving.append(copy)
    for copy in leaving:
        copy.wait()


def on_device(
    mamba_in, mamba_gate, conv_weight, conv_bias, proj_delta, proj_select, delta_weight, delta_bias, decay_log, skip_gain,
):
    rows, width = mamba_in.shape
    rank = proj_delta.shape[1]
    maps = proj_select.shape[1]
    halves = width // LANES
    steps = rows // CHUNKS
    n_ctx, n_ch = lax.axis_size("ctx"), lax.axis_size("ch")
    wide = rank + LANES
    cells = rows * width * STATE
    tile = jax.ShapeDtypeStruct((rows, width), F32)
    near = n_ch // 2
    tall = OWN * rank // LANES + OWN // 2
    part_shape = jax.ShapeDtypeStruct((near, tall, LANES), BF16)
    big = pltpu.VMEM((rows, STATE * LANES), F32)

    halo = lax.ppermute(mamba_in[rows - 16 :], "ctx", [(i, i + 1) for i in range(n_ctx - 1)])
    act, part, head, pd, sel, taps = pl.pallas_call(
        project_kernel,
        out_shape=(
            tile,
            part_shape,
            jax.ShapeDtypeStruct((8, width), F32),
            jax.ShapeDtypeStruct(proj_delta.shape, BF16),
            jax.ShapeDtypeStruct((LANES, width), BF16),
            jax.ShapeDtypeStruct((8, width), F32),
        ),
        in_specs=hbm(5),
        out_specs=tuple(vmem(6)),
        scratch_shapes=[
            pltpu.VMEM((rows, width), BF16),
            pltpu.VMEM((KWIDTH, width), F32),
            pltpu.VMEM((1, width), F32),
            pltpu.VMEM((maps, width), BF16),
            pltpu.VMEM((halves, rows + 8, LANES), F32),
            pltpu.VMEM((halves, (steps + KWIDTH - 1) * CHUNKS, LANES), F32),
            pltpu.VMEM((rows, width), BF16),
            pltpu.VMEM((rows, rank), F32),
            pltpu.VMEM((rows, LANES), F32),
            pltpu.SemaphoreType.DMA((5,)),
        ],
        compiler_params=pltpu.CompilerParams(vmem_limit_bytes=16 * MIB),
        cost_estimate=pl.CostEstimate(
            flops=2 * rows * width * wide, bytes_accessed=2 * rows * width * 8, transcendentals=rows * width
        ),
        name="project",
    )(
        *stay(
            mamba_in, proj_delta, proj_select.T, conv_weight, conv_bias[None, :],
        )
    )
    act, part = pl.pallas_call(
        functools.partial(head_kernel, maps),
        out_shape=(tile, part_shape),
        in_specs=vmem(7),
        out_specs=tuple(vmem(2)),
        scratch_shapes=[
            pltpu.VMEM((16, width), F32),
            pltpu.VMEM((HEAD, rank), F32),
            pltpu.VMEM((HEAD, LANES), F32),
        ],
        compiler_params=pltpu.CompilerParams(vmem_limit_bytes=16 * MIB),
        name="first_rows",
    )(halo, head, taps, pd, sel, act, part)

    groups = [list(range(near)), list(range(near, n_ch))]
    parts = lax.all_to_all(part, "ch", 0, 0, axis_index_groups=groups)
    mine, send = pl.pallas_call(
        functools.partial(total_kernel, maps),
        out_shape=tuple(jax.ShapeDtypeStruct((tall + OWN // 2, LANES), kind) for kind in (F32, BF16)),
        in_specs=vmem(1),
        out_specs=tuple(vmem(2)),
        compiler_params=pltpu.CompilerParams(vmem_limit_bytes=16 * MIB),
        name="total",
    )(parts)
    other = lax.ppermute(send, "ch", [(i, (i + near) % n_ch) for i in range(n_ch)])
    lit, spread, done, dw, rate, vecs = pl.pallas_call(
        ready_kernel,
        out_shape=(
            tile,
            jax.ShapeDtypeStruct((LANES, STATE * LANES), BF16),
            jax.ShapeDtypeStruct((8, LANES), F32),
            jax.ShapeDtypeStruct(delta_weight.shape, BF16),
            jax.ShapeDtypeStruct((STATE, width), F32),
            jax.ShapeDtypeStruct((8, width), F32),
        ),
        in_specs=vmem(1) + hbm(4),
        out_specs=tuple(vmem(6)),
        scratch_shapes=[
            pltpu.VMEM((rows, width), BF16),
            pltpu.VMEM((STATE, width), F32),
            pltpu.SemaphoreType.DMA((4,)),
        ],
        compiler_params=pltpu.CompilerParams(vmem_limit_bytes=16 * MIB),
        cost_estimate=pl.CostEstimate(
            flops=16 * rows * width, bytes_accessed=8 * rows * width, transcendentals=rows * width
        ),
        name="ready",
    )(mine, *stay(mamba_gate, delta_weight, decay_log, delta_bias[None, :]))
    totals = pl.pallas_call(
        functools.partial(share_kernel, maps),
        out_shape=jax.ShapeDtypeStruct(parts.shape, BF16),
        in_specs=vmem(3),
        out_specs=vmem(1)[0],
        compiler_params=pltpu.CompilerParams(vmem_limit_bytes=16 * MIB),
        name="share",
    )(mine, other, done)
    gathered = lax.all_to_all(totals, "ch", 0, 0, axis_index_groups=groups)

    sent = (
        ((rows, width), F32),
        ((STATE, CHUNKS, width), F32),
        ((CHUNKS, width), F32),
        ((rows, LANES), BF16),
        ((n_ctx, halves * STATE + CHUNKS, LANES), BF16),
    )
    delta, inside, before, maps_all, pay = pl.pallas_call(
        ends_kernel,
        out_shape=tuple(pltpu.HBM(*kept) for kept in sent),
        in_specs=vmem(6),
        out_specs=tuple(hbm(5)),
        scratch_shapes=[
            *(pltpu.VMEM(*kept) for kept in sent),
            pltpu.VMEM((rows, rank), BF16),
            pltpu.VMEM((rows, width), F32),
            big,
            pltpu.VMEM((rows, width), F32),
            pltpu.VMEM((STATE + 8, width), F32),
            pltpu.SemaphoreType.DMA((5,)),
        ],
        compiler_params=pltpu.CompilerParams(vmem_limit_bytes=16 * MIB),
        name="ends",
    )(gathered, act, dw, vecs, rate, spread)

    got = lax.all_to_all(pay, "ctx", 0, 0)
    y_local, cum, turned = pl.pallas_call(
        local_kernel,
        out_shape=(
            tile,
            tile,
            jax.ShapeDtypeStruct((rows, LANES), BF16),
        ),
        in_specs=vmem(3) + hbm(5),
        out_specs=tuple(vmem(3)),
        scratch_shapes=[
            big,
            big,
            *(pltpu.VMEM(*kept) for kept in sent[:4]),
            pltpu.VMEM((1, width), F32),
            pltpu.SemaphoreType.DMA((5,)),
        ],
        compiler_params=pltpu.CompilerParams(vmem_limit_bytes=24 * MIB),
        cost_estimate=pl.CostEstimate(flops=6 * cells, bytes_accessed=8 * rows * width * 4, transcendentals=cells),
        name="local_scan",
    )(act, rate, spread, *stay(delta, inside, before, maps_all, skip_gain[None, :]))
    return pl.pallas_call(
        finish_kernel,
        out_shape=jax.ShapeDtypeStruct((rows, width), BF16),
        in_specs=vmem(7),
        out_specs=hbm(1)[0],
        scratch_shapes=[
            big,
            pltpu.VMEM((STATE, width), F32),
            pltpu.VMEM((halves, rows, LANES), F32),
            pltpu.VMEM((halves, rows, LANES), BF16),
            pltpu.SemaphoreType.DMA((halves,)),
        ],
        compiler_params=pltpu.CompilerParams(vmem_limit_bytes=16 * MIB),
        name="finish",
    )(got, turned, spread, y_local, cum, rate, lit)


def solution(mesh):
    return jax.shard_map(
        on_device,
        mesh=mesh,
        in_specs=(
            P("ctx", "ch"),
            P("ctx", "ch"),
            P(None, "ch"),
            P("ch"),
            P("ch", None),
            P("ch", None),
            P(None, "ch"),
            P("ch"),
            P(None, "ch"),
            P("ch"),
        ),
        out_specs=P("ctx", "ch"),
        check_vma=False,
    )
```

```python
import functools
import math

import jax
import jax.numpy as jnp
from jax import lax
from jax.experimental import pallas as pl
from jax.experimental.pallas import tpu as pltpu
from jax.sharding import PartitionSpec as P

STATE = 16
KWIDTH = 4
LANES = 128
CHUNKS = 8
OWN = 16
HEAD = 32
LOG2E = 1.0 / math.log(2.0)
MIB = 1 << 20
F32 = jnp.float32
BF16 = jnp.bfloat16


def vmem(count):
    return [pl.BlockSpec(memory_space=pltpu.VMEM)] * count


def hbm(count):
    return [pl.BlockSpec(memory_space=pltpu.HBM)] * count


def stay(*arrays):
    return [pltpu.with_memory_space_constraint(array, pltpu.HBM) for array in arrays]


def silu(value):
    return value / (1.0 + jnp.exp(-value))


def pack(low, first, second):
    pieces = [low[:, at : at + LANES] for at in range(0, low.shape[1], LANES)]
    return jnp.concatenate(pieces + [first + pltpu.roll(second, LANES // 2, 1)], axis=0).astype(BF16)


def put_products(low, pd, sel, maps, part_ref, products, chosen):
    rows = low.shape[0]
    products[0:rows, :] = jnp.dot(low, pd, preferred_element_type=F32)
    both = lax.dot_general(low, sel, (((1,), (1,)), ((), ())), preferred_element_type=F32)
    high = both.astype(BF16).astype(F32)
    lane = lax.broadcasted_iota(jnp.int32, both.shape, 1)
    chosen[0:rows, :] = jnp.where(lane < maps, high, both - high)
    for block in range(rows // OWN):
        at = block * OWN
        part_ref[block] = pack(
            products[at : at + OWN, :], chosen[at : at + OWN // 2, :], chosen[at + OWN // 2 : at + OWN, :]
        )


def project_kernel(
    x_hbm, pd_hbm, ps_hbm, weight_hbm, bias_hbm,
    act_ref, part_ref, head_ref, pd_ref, sel_ref, taps_ref,
    x_ref, weight_ref, bias_ref, ps_ref, xs, xp, low, products, chosen, sems,
):
    rows, width = x_ref.shape
    steps = rows // CHUNKS
    maps = ps_ref.shape[0]
    halves = width // LANES
    pairs = (
        (x_hbm, x_ref), (weight_hbm, weight_ref), (bias_hbm, bias_ref), (ps_hbm, ps_ref), (pd_hbm, pd_ref),
    )
    copies = [pltpu.make_async_copy(source, target, sems.at[i]) for i, (source, target) in enumerate(pairs)]
    for copy in copies:
        copy.start()
    copies[0].wait()
    head_ref[...] = x_ref[0:16, :].astype(F32)[0:8, :]
    for half in range(halves):
        cols = slice(half * LANES, (half + 1) * LANES)
        xs[half, 0:8, :] = jnp.zeros((8, LANES), F32)
        xs[half, 8 : 8 + rows, :] = x_ref[:, cols].astype(F32)
        for step in range(-(KWIDTH - 1), steps):
            to = (step + KWIDTH - 1) * CHUNKS
            xp[half, to : to + CHUNKS, :] = xs[half, pl.ds(8 + step, CHUNKS, stride=steps), :]
    copies[1].wait()
    copies[2].wait()
    taps_ref[0:KWIDTH, :] = weight_ref[...]
    taps_ref[KWIDTH : KWIDTH + 1, :] = bias_ref[...]
    block = min(rows, 64)
    for half in range(halves):
        cols = slice(half * LANES, (half + 1) * LANES)
        for start in range(0, rows, block):
            value = bias_ref[:, cols]
            for tap in range(KWIDTH):
                at = start + tap * CHUNKS
                value = value + weight_ref[tap : tap + 1, cols] * xp[half, at : at + block, :]
            value = silu(value)
            act_ref[start : start + block, cols] = value
            low[start : start + block, cols] = value.astype(BF16)
    copies[3].wait()
    sel_ref[...] = jnp.zeros_like(sel_ref)
    sel_ref[0:maps, :] = ps_ref[...]
    sel_ref[maps : 2 * maps, :] = ps_ref[...]
    copies[4].wait()
    put_products(low[...], pd_ref[...], sel_ref[...], maps, part_ref, products, chosen)


def head_kernel(maps, halo_ref, head_ref, taps_ref, pd_ref, sel_ref, act_in, part_in, act_ref, part_ref, ext, products, chosen):
    ext[0:8, :] = halo_ref[...].astype(F32)[-8:, :]
    ext[8:16, :] = head_ref[...]
    value = taps_ref[KWIDTH : KWIDTH + 1, :]
    for tap in range(KWIDTH):
        at = 8 - (KWIDTH - 1) + tap
        value = value + taps_ref[tap : tap + 1, :] * ext[at : at + 8, :]
    value = silu(value)
    act_ref[...] = act_in[...]
    part_ref[...] = part_in[...]
    for token in range(KWIDTH - 1):
        act_ref[token * CHUNKS : token * CHUNKS + 1, :] = value[token : token + 1, :]
    low = act_ref[0:HEAD, :].astype(BF16)
    put_products(low, pd_ref[...], sel_ref[...], maps, part_ref, products, chosen)


def fold(chosen, maps):
    lane = lax.broadcasted_iota(jnp.int32, chosen.shape, 1)
    summed = chosen + pltpu.roll(chosen, LANES - maps, 1)
    twice = jnp.where(lane < maps, summed, pltpu.roll(summed, maps, 1))
    return jnp.where(lane < 2 * maps, twice, 0.0)


def parted(twice, maps):
    lane = lax.broadcasted_iota(jnp.int32, twice.shape, 1)
    high = twice.astype(BF16).astype(F32)
    return jnp.where(lane < maps, high, twice - high)


def total_kernel(maps, parts_ref, mine_ref, send_ref):
    total = parts_ref[0].astype(F32)
    for source in range(1, parts_ref.shape[0]):
        total = total + parts_ref[source].astype(F32)
    cut = total.shape[0] - OWN // 2
    low, packed = total[:cut, :], total[cut:, :]
    twice = jnp.concatenate([fold(packed, maps), fold(pltpu.roll(packed, LANES // 2, 1), maps)], axis=0)
    mine_ref[...] = jnp.concatenate([low, twice], axis=0)
    send_ref[...] = jnp.concatenate([low, parted(twice, maps)], axis=0).astype(BF16)


def share_kernel(maps, mine_ref, other_ref, ready_ref, out_ref):
    cut = mine_ref.shape[0] - OWN
    other = other_ref[...].astype(F32)
    low = mine_ref[:cut, :] + other[:cut, :]
    twice = parted(mine_ref[cut:, :] + fold(other[cut:, :], maps), maps)
    packed = twice[: OWN // 2, :] + pltpu.roll(twice[OWN // 2 :, :], LANES // 2, 1)
    block = jnp.concatenate([low, packed], axis=0).astype(BF16)
    for target in range(out_ref.shape[0]):
        out_ref[target] = block


def ready_kernel(
    mine_ref, gate_hbm, dw_hbm, log_hbm, bias_hbm,
    lit_ref, spread_ref, done_ref, dw_ref, rate_ref, bias_ref,
    gate_ref, log_ref, sems,
):
    pairs = ((gate_hbm, gate_ref), (dw_hbm, dw_ref), (log_hbm, log_ref), (bias_hbm, bias_ref.at[0:1]))
    copies = [pltpu.make_async_copy(source, target, sems.at[i]) for i, (source, target) in enumerate(pairs)]
    for copy in copies:
        copy.start()
    source = lax.broadcasted_iota(jnp.int32, spread_ref.shape, 0)
    group = lax.broadcasted_iota(jnp.int32, spread_ref.shape, 1) >> 7
    hit = (source == group) | (source == group + 2 * STATE)
    spread_ref[...] = jnp.where(hit, 1.0, 0.0).astype(BF16)
    done_ref[...] = jnp.zeros_like(done_ref)
    for copy in copies:
        copy.wait()
    rate_ref[...] = -jnp.exp(log_ref[...]) * LOG2E
    lit_ref[...] = silu(gate_ref[...].astype(F32))


def step_rows(step):
    return pl.ds(pl.multiple_of(step * CHUNKS, CHUNKS), CHUNKS)


def unpack_maps(g_ref, maps_ref):
    for block in range(g_ref.shape[0]):
        packed = g_ref[block].astype(F32)[-(OWN // 2) :, :]
        both = jnp.concatenate([packed, pltpu.roll(packed, LANES // 2, 1)], axis=0)
        maps_ref[block * OWN : (block + 1) * OWN, :] = both.astype(BF16)


def ends_kernel(
    g_ref, act_ref, dw_ref, vecs_ref, rate, spread_ref,
    delta_hbm, inside_hbm, before_hbm, pay_hbm,
    delta, inside_ref, before_ref, pay_ref, maps_ref, low, drive, b_all, cum_ref, ends, sems,
):
    rows, width = act_ref.shape
    steps = rows // CHUNKS
    halves = width // LANES
    for block in range(g_ref.shape[0]):
        at = slice(block * OWN, (block + 1) * OWN)
        for piece in range(low.shape[1] // LANES):
            low[at, piece * LANES : (piece + 1) * LANES] = g_ref[block, piece * OWN : (piece + 1) * OWN, :]
    unpack_maps(g_ref, maps_ref)
    z = jnp.dot(low[...], dw_ref[...], preferred_element_type=F32) + vecs_ref[0:1, :]
    step_size = jnp.maximum(z, 0.0) + jnp.log1p(jnp.exp(-jnp.abs(z)))
    delta[...] = step_size
    pairs = (
        (delta, delta_hbm), (inside_ref, inside_hbm), (before_ref, before_hbm), (pay_ref, pay_hbm),
    )
    copies = [pltpu.make_async_copy(source, target, sems.at[i]) for i, (source, target) in enumerate(pairs)]
    copies[0].start()
    drive[...] = step_size * act_ref[...]
    b_all[...] = jnp.dot(maps_ref[...], spread_ref[...], preferred_element_type=F32)
    chunk = lax.broadcasted_iota(jnp.int32, (CHUNKS, LANES), 0)
    zero = jnp.zeros((CHUNKS, LANES), F32)

    def add(step, totals):
        at = step_rows(step)
        totals = [totals[half] + delta[at, half * LANES : (half + 1) * LANES] for half in range(halves)]
        for half in range(halves):
            cum_ref[at, half * LANES : (half + 1) * LANES] = totals[half]
        return totals

    totals = lax.fori_loop(0, steps, add, [zero] * halves, unroll=8)
    for half in range(halves):
        cols = slice(half * LANES, (half + 1) * LANES)
        rates = [jnp.broadcast_to(rate[n : n + 1, cols], (CHUNKS, LANES)) for n in range(STATE)]
        total = totals[half]

        def gather(step, states, cols=cols, rates=rates, total=total):
            at = step_rows(step)
            left = total - cum_ref[at, cols]
            push = drive[at, cols]
            return [
                states[n] + jnp.exp2(left * rates[n]) * (push * b_all[at, n * LANES : (n + 1) * LANES])
                for n in range(STATE)
            ]

        states = lax.fori_loop(0, steps, gather, [zero] * STATE, unroll=16)
        sums = [total]
        shift = 1
        while shift < CHUNKS:
            sums.append(sums[-1] + jnp.where(chunk >= shift, pltpu.roll(sums[-1], shift, 0), 0.0))
            shift *= 2
        for n in range(STATE):
            end = states[n]
            shift = 1
            for level in range(len(sums) - 1):
                end = end + jnp.exp2(rates[n] * sums[level]) * jnp.where(
                    chunk >= shift, pltpu.roll(end, shift, 0), 0.0
                )
                shift *= 2
            inside_ref[n, :, cols] = jnp.where(chunk >= 1, pltpu.roll(end, 1, 0), 0.0)
            ends[n : n + 1, cols] = end[CHUNKS - 1 :, :]
        before_ref[:, cols] = jnp.where(chunk >= 1, pltpu.roll(sums[-1], 1, 0), 0.0)
        ends[STATE : STATE + 1, cols] = sums[-1][CHUNKS - 1 :, :]

    copies[1].start()
    copies[2].start()
    me = lax.axis_index("ctx")
    row = lax.broadcasted_iota(jnp.int32, (CHUNKS, LANES), 0)
    pieces, tail = [], zero
    for half in range(halves):
        cols = slice(half * LANES, (half + 1) * LANES)
        pieces.append(ends[0:STATE, cols])
        total = jnp.broadcast_to(ends[STATE : STATE + 1, cols], tail.shape)
        high = total.astype(BF16).astype(F32)
        tail = jnp.where(row == 2 * half, high, jnp.where(row == 2 * half + 1, total - high, tail))
    block = jnp.concatenate(pieces + [tail], axis=0)
    for target in range(pay_ref.shape[0]):
        pay_ref[target] = jnp.where(target > me, block, 0.0).astype(BF16)
    copies[3].start()
    for copy in copies:
        copy.wait()


def local_kernel(
    g_ref, act_ref, rate, spread_ref, delta_hbm, inside_hbm, before_hbm, gain_hbm,
    y_ref, cum_ref, maps_ref,
    b_all, c_all, delta, inside_ref, before_ref, both_ref, gain_ref, sems,
):
    rows, width = act_ref.shape
    steps = rows // CHUNKS
    halves = width // LANES
    pairs = (
        (delta_hbm, delta), (inside_hbm, inside_ref), (before_hbm, before_ref), (gain_hbm, gain_ref),
    )
    copies = [pltpu.make_async_copy(source, target, sems.at[i]) for i, (source, target) in enumerate(pairs)]
    for copy in copies:
        copy.start()
    unpack_maps(g_ref, both_ref)
    maps = both_ref[...]
    b_all[...] = jnp.dot(maps, spread_ref[...], preferred_element_type=F32)
    maps_ref[...] = pltpu.roll(maps.astype(F32), LANES - STATE, 1).astype(BF16)
    c_all[...] = jnp.dot(maps_ref[...], spread_ref[...], preferred_element_type=F32)
    for copy in copies:
        copy.wait()
    for half in range(halves):
        cols = slice(half * LANES, (half + 1) * LANES)
        rates = [jnp.broadcast_to(rate[n : n + 1, cols], (CHUNKS, LANES)) for n in range(STATE)]
        gain = gain_ref[:, cols]

        def advance(step, carried, cols=cols, rates=rates, gain=gain):
            states, total = carried
            at = step_rows(step)
            size = delta[at, cols]
            value = act_ref[at, cols]
            push = size * value
            total = total + size
            out = gain * value
            later = []
            for n in range(STATE):
                group = slice(n * LANES, (n + 1) * LANES)
                now = jnp.exp2(size * rates[n]) * states[n] + push * b_all[at, group]
                out = out + c_all[at, group] * now
                later.append(now)
            y_ref[at, cols] = out
            cum_ref[at, cols] = total
            return later, total

        lax.fori_loop(
            0, steps, advance, ([inside_ref[n, :, cols] for n in range(STATE)], before_ref[:, cols]), unroll=8
        )


def finish_kernel(got_ref, maps_ref, spread_ref, y_ref, cum_ref, rate, lit_ref, out_hbm, c_all, carry, ys, out_ref, sems):
    rows, width = y_ref.shape
    steps = rows // CHUNKS
    halves = width // LANES
    c_all[...] = jnp.dot(maps_ref[...], spread_ref[...], preferred_element_type=F32)
    incoming = [jnp.zeros((STATE, LANES), F32)] * halves
    for source in range(got_ref.shape[0] - 1):
        block = got_ref[source].astype(F32)
        tail = block[halves * STATE :, :]
        for half in range(halves):
            total = tail[2 * half : 2 * half + 1, :] + tail[2 * half + 1 : 2 * half + 2, :]
            decay = jnp.exp2(rate[:, half * LANES : (half + 1) * LANES] * total)
            incoming[half] = decay * incoming[half] + block[half * STATE : (half + 1) * STATE, :]
    for half in range(halves):
        carry[:, half * LANES : (half + 1) * LANES] = incoming[half]
    leaving = []
    for half in range(halves):
        cols = slice(half * LANES, (half + 1) * LANES)
        rates = [jnp.broadcast_to(rate[n : n + 1, cols], (CHUNKS, LANES)) for n in range(STATE)]
        entering = [jnp.broadcast_to(carry[n : n + 1, cols], (CHUNKS, LANES)) for n in range(STATE)]

        def correct(step, _, half=half, cols=cols, rates=rates, entering=entering):
            at = step_rows(step)
            total = cum_ref[at, cols]
            out = y_ref[at, cols]
            for n in range(STATE):
                group = slice(n * LANES, (n + 1) * LANES)
                out = out + (c_all[at, group] * entering[n]) * jnp.exp2(total * rates[n])
            ys[half, pl.ds(step, CHUNKS, stride=steps), :] = out
            return 0

        lax.fori_loop(0, steps, correct, 0, unroll=16)
        out_ref[half] = (ys[half] * lit_ref[:, cols]).astype(BF16)
        copy = pltpu.make_async_copy(out_ref.at[half], out_hbm.at[:, cols], sems.at[half])
        copy.start()
        leaving.append(copy)
    for copy in leaving:
        copy.wait()


def on_device(
    mamba_in, mamba_gate, conv_weight, conv_bias, proj_delta, proj_select, delta_weight, delta_bias, decay_log, skip_gain,
):
    rows, width = mamba_in.shape
    rank = proj_delta.shape[1]
    maps = proj_select.shape[1]
    halves = width // LANES
    steps = rows // CHUNKS
    n_ctx, n_ch = lax.axis_size("ctx"), lax.axis_size("ch")
    wide = rank + LANES
    cells = rows * width * STATE
    tile = jax.ShapeDtypeStruct((rows, width), F32)
    near = n_ch // 2
    tall = OWN * rank // LANES + OWN // 2
    part_shape = jax.ShapeDtypeStruct((near, tall, LANES), BF16)
    big = pltpu.VMEM((rows, STATE * LANES), F32)

    halo = lax.ppermute(mamba_in[rows - 16 :], "ctx", [(i, i + 1) for i in range(n_ctx - 1)])
    act, part, head, pd, sel, taps = pl.pallas_call(
        project_kernel,
        out_shape=(
            tile,
            part_shape,
            jax.ShapeDtypeStruct((8, width), F32),
            jax.ShapeDtypeStruct(proj_delta.shape, BF16),
            jax.ShapeDtypeStruct((LANES, width), BF16),
            jax.ShapeDtypeStruct((8, width), F32),
        ),
        in_specs=hbm(5),
        out_specs=tuple(vmem(6)),
        scratch_shapes=[
            pltpu.VMEM((rows, width), BF16),
            pltpu.VMEM((KWIDTH, width), F32),
            pltpu.VMEM((1, width), F32),
            pltpu.VMEM((maps, width), BF16),
            pltpu.VMEM((halves, rows + 8, LANES), F32),
            pltpu.VMEM((halves, (steps + KWIDTH - 1) * CHUNKS, LANES), F32),
            pltpu.VMEM((rows, width), BF16),
            pltpu.VMEM((rows, rank), F32),
            pltpu.VMEM((rows, LANES), F32),
            pltpu.SemaphoreType.DMA((5,)),
        ],
        compiler_params=pltpu.CompilerParams(vmem_limit_bytes=16 * MIB),
        cost_estimate=pl.CostEstimate(
            flops=2 * rows * width * wide, bytes_accessed=2 * rows * width * 8, transcendentals=rows * width
        ),
        name="project",
    )(
        *stay(
            mamba_in, proj_delta, proj_select.T, conv_weight, conv_bias[None, :],
        )
    )
    act, part = pl.pallas_call(
        functools.partial(head_kernel, maps),
        out_shape=(tile, part_shape),
        in_specs=vmem(7),
        out_specs=tuple(vmem(2)),
        scratch_shapes=[
            pltpu.VMEM((16, width), F32),
            pltpu.VMEM((HEAD, rank), F32),
            pltpu.VMEM((HEAD, LANES), F32),
        ],
        compiler_params=pltpu.CompilerParams(vmem_limit_bytes=16 * MIB),
        name="first_rows",
    )(halo, head, taps, pd, sel, act, part)

    groups = [list(range(near)), list(range(near, n_ch))]
    parts = lax.all_to_all(part, "ch", 0, 0, axis_index_groups=groups)
    mine, send = pl.pallas_call(
        functools.partial(total_kernel, maps),
        out_shape=tuple(jax.ShapeDtypeStruct((tall + OWN // 2, LANES), kind) for kind in (F32, BF16)),
        in_specs=vmem(1),
        out_specs=tuple(vmem(2)),
        compiler_params=pltpu.CompilerParams(vmem_limit_bytes=16 * MIB),
        name="total",
    )(parts)
    other = lax.ppermute(send, "ch", [(i, (i + near) % n_ch) for i in range(n_ch)])
    lit, spread, done, dw, rate, vecs = pl.pallas_call(
        ready_kernel,
        out_shape=(
            tile,
            jax.ShapeDtypeStruct((LANES, STATE * LANES), BF16),
            jax.ShapeDtypeStruct((8, LANES), F32),
            jax.ShapeDtypeStruct(delta_weight.shape, BF16),
            jax.ShapeDtypeStruct((STATE, width), F32),
            jax.ShapeDtypeStruct((8, width), F32),
        ),
        in_specs=vmem(1) + hbm(4),
        out_specs=tuple(vmem(6)),
        scratch_shapes=[
            pltpu.VMEM((rows, width), BF16),
            pltpu.VMEM((STATE, width), F32),
            pltpu.SemaphoreType.DMA((4,)),
        ],
        compiler_params=pltpu.CompilerParams(vmem_limit_bytes=16 * MIB),
        cost_estimate=pl.CostEstimate(
            flops=16 * rows * width, bytes_accessed=8 * rows * width, transcendentals=rows * width
        ),
        name="ready",
    )(mine, *stay(mamba_gate, delta_weight, decay_log, delta_bias[None, :]))
    totals = pl.pallas_call(
        functools.partial(share_kernel, maps),
        out_shape=jax.ShapeDtypeStruct(parts.shape, BF16),
        in_specs=vmem(3),
        out_specs=vmem(1)[0],
        compiler_params=pltpu.CompilerParams(vmem_limit_bytes=16 * MIB),
        name="share",
    )(mine, other, done)
    gathered = lax.all_to_all(totals, "ch", 0, 0, axis_index_groups=groups)

    sent = (
        ((rows, width), F32),
        ((STATE, CHUNKS, width), F32),
        ((CHUNKS, width), F32),
        ((n_ctx, halves * STATE + CHUNKS, LANES), BF16),
    )
    delta, inside, before, pay = pl.pallas_call(
        ends_kernel,
        out_shape=tuple(pltpu.HBM(*kept) for kept in sent),
        in_specs=vmem(6),
        out_specs=tuple(hbm(4)),
        scratch_shapes=[
            *(pltpu.VMEM(*kept) for kept in sent),
            pltpu.VMEM((rows, LANES), BF16),
            pltpu.VMEM((rows, rank), BF16),
            pltpu.VMEM((rows, width), F32),
            big,
            pltpu.VMEM((rows, width), F32),
            pltpu.VMEM((STATE + 8, width), F32),
            pltpu.SemaphoreType.DMA((4,)),
        ],
        compiler_params=pltpu.CompilerParams(vmem_limit_bytes=16 * MIB),
        name="ends",
    )(gathered, act, dw, vecs, rate, spread)

    got = lax.all_to_all(pay, "ctx", 0, 0)
    y_local, cum, turned = pl.pallas_call(
        local_kernel,
        out_shape=(
            tile,
            tile,
            jax.ShapeDtypeStruct((rows, LANES), BF16),
        ),
        in_specs=vmem(4) + hbm(4),
        out_specs=tuple(vmem(3)),
        scratch_shapes=[
            big,
            big,
            *(pltpu.VMEM(*kept) for kept in sent[:3]),
            pltpu.VMEM((rows, LANES), BF16),
            pltpu.VMEM((1, width), F32),
            pltpu.SemaphoreType.DMA((4,)),
        ],
        compiler_params=pltpu.CompilerParams(vmem_limit_bytes=24 * MIB),
        cost_estimate=pl.CostEstimate(flops=6 * cells, bytes_accessed=8 * rows * width * 4, transcendentals=cells),
        name="local_scan",
    )(gathered, act, rate, spread, *stay(delta, inside, before, skip_gain[None, :]))
    return pl.pallas_call(
        finish_kernel,
        out_shape=jax.ShapeDtypeStruct((rows, width), BF16),
        in_specs=vmem(7),
        out_specs=hbm(1)[0],
        scratch_shapes=[
            big,
            pltpu.VMEM((STATE, width), F32),
            pltpu.VMEM((halves, rows, LANES), F32),
            pltpu.VMEM((halves, rows, LANES), BF16),
            pltpu.SemaphoreType.DMA((halves,)),
        ],
        compiler_params=pltpu.CompilerParams(vmem_limit_bytes=16 * MIB),
        name="finish",
    )(got, turned, spread, y_local, cum, rate, lit)


def solution(mesh):
    return jax.shard_map(
        on_device,
        mesh=mesh,
        in_specs=(
            P("ctx", "ch"),
            P("ctx", "ch"),
            P(None, "ch"),
            P("ch"),
            P("ch", None),
            P("ch", None),
            P(None, "ch"),
            P("ch"),
            P(None, "ch"),
            P("ch"),
        ),
        out_specs=P("ctx", "ch"),
        check_vma=False,
    )
```
